32 devices in a mesh: expert: 8 (over y, x, core), chan: 4 (over z).
Axes of the slice: x: 2, y: 2, z: 4, core: 2. Of those that a mesh axis runs over, the one named last changes fastest.
Arguments:
- tiles_in: bfloat16 [64, 3, 3, 2048], P('expert', None, None, 'chan'), may hold values from -6 to 6
- grad_out: bfloat16 [64, 3, 3, 2048], P('expert', None, None, 'chan'), may hold values from -6 to 6
- gate: bfloat16 [64], P('expert'), may hold values from 0.19921875 to 1
- expert_id: int32 [64, 1], P('expert'), may hold values from 0 to 7; in each aligned block of 8 rows (0 to 7, 8 to 15, ...) at most 2 rows name the same one
- w_conv: bfloat16 [8, 3, 3, 32, 16384], P('expert', None, None, None, 'chan'), may hold values from -0.375 to 0.375
- w_depth: bfloat16 [8, 9, 16384], P('expert', None, 'chan'), may hold values from -2 to 2
- w_out: bfloat16 [8, 16384, 2048], P('expert', 'chan'), may hold values from -0.046875 to 0.046875
Outputs:
- grad_input: bfloat16 [64, 3, 3, 2048], P('expert', None, None, 'chan')
- grad_gate: bfloat16 [64], P('expert')
The draws below stay inside these ranges and needn't reach their ends.
Inputs may be any that keep to these rules, and one draw needn't show every extreme that they name: `expert_id`: within the 8 tiles of one index of expert, no expert is named more than 2 times, and in every draw some expert is named exactly 2 times there.
All inputs are finite; a program needn't handle non-finite values.
Results may differ from the reference program's by a relative error of at most 0.009.
Values may be sent and summed in bfloat16 or wider, within the bound.
A program may use at most 64 MiB of HBM per device.

```python
import math
import jax
import jax.numpy as jnp
import numpy as np
from jax import lax

D = 2048
F = 16384
GROUPS = 64
TS = 3
CAP = 2
TILES_DEV = 8
EXPERTS = 8
TILES = 64
DG = 32
N_EXPERT = 8


def levels(own_key, dims, cuts, smallest, largest):
    factor_of, own = 1.0, jax.random.fold_in(own_key, 6)
    for dim, blocks in cuts:
        heights = jnp.exp(jax.random.uniform(jax.random.fold_in(own, dim), (blocks,), jnp.float32, smallest / len(cuts), largest / len(cuts)))
        factor_of = factor_of * jnp.repeat(heights, dims[dim] // blocks).reshape([-1 if axis == dim else 1 for axis in range(len(dims))])
    return factor_of


def deal_out(stream_key, own, number, rows, count, top, limit, slope):
    order = jax.random.permutation(stream_key, count)
    heavy_load, common = load_shares(count, rows * top, limit, slope, True), load_shares(count, rows * top, limit, slope, False)
    places = jnp.arange(count)

    def named(lengths, turn):
        used = int((lengths > 0).sum())
        fixed = max(1, used // 4)
        passed = fixed + (places - fixed + turn * (used - fixed)) % max(1, count - fixed)
        return jnp.zeros((count,), jnp.int32).at[order[jnp.where(places < fixed, places, passed)]].set(jnp.asarray(lengths, jnp.int32))

    lengths = jnp.where(number % 4 == 0, named(heavy_load, number // 4), named(common, number - number // 4 - 1))
    mixed = jax.random.permutation(jax.random.fold_in(own, 3), count)
    source_of, taker = mixed[0:count // 2 * 2:2], mixed[1:count // 2 * 2:2]
    margin = jnp.minimum(lengths[source_of] - 1, limit - lengths[taker]) // 2
    margin = jnp.where((source_of == order[0]) | (taker == order[0]) | (lengths[taker] == 0), 0, jnp.maximum(margin, 0))
    passed = jax.random.randint(jax.random.fold_in(own, 4), (count // 2,), 0, 1 << 20) % (margin + 1)
    lengths = lengths.at[source_of].add(-passed).at[taker].add(passed)
    members = jnp.searchsorted(jnp.cumsum(lengths), jnp.arange(rows * top), side="right").astype(jnp.int32)
    table = members.reshape(top, rows).T
    table = table[jax.random.permutation(jax.random.fold_in(own, 1), rows)]
    turn = jax.random.randint(jax.random.fold_in(own, 2), (rows, 1), 0, top)
    return jnp.take_along_axis(table, (jnp.arange(top)[None, :] + turn) % top, axis=1)


def load_shares(number_of, total, most, skew, full):
    weights = [(1 << 20) // math.isqrt(standing ** skew) + 1 for standing in range(1, number_of + 1)]
    largest = most if full else min(most, max(-(-total // number_of), total * weights[0] // sum(weights)))
    least = 1 if total - largest >= number_of - 1 else 0
    counts, surplus = [largest] + [least] * (number_of - 1), total - largest - least * (number_of - 1)
    while surplus > 0:
        candidates = [i for i in range(1, number_of) if counts[i] < largest] or [i for i in range(1, number_of) if counts[i] < most]
        mass, budget = sum([weights[i] for i in candidates]), surplus
        for i in candidates:
            addition = min(most - counts[i], max(1, budget * weights[i] // mass), surplus)
            counts[i] = counts[i] + addition
            surplus = surplus - addition
    return np.array(counts)


def gaussian(rng, dims, width, most, shards=(), kind=jnp.bfloat16):
    array = width * jax.random.normal(rng, dims, jnp.float32)
    if shards:
        array = array * levels(rng, dims, shards, -0.22, 0.18)
    return jnp.clip(array, -most, most).astype(kind)


def setup_inputs(seed: int = 0) -> dict:
    streams_of = jax.random.split(jax.random.key(seed), 8)
    tiles_in = gaussian(streams_of[0], (TILES, TS, TS, D), 1.0, 6.0, ((0, 8), (3, 4)))
    grad_out = gaussian(streams_of[1], (TILES, TS, TS, D), 1.0, 6.0, ((0, 8), (3, 4)))
    gate = jnp.clip(jnp.exp(math.log(1.0) - 1.6133518 * jax.random.uniform(streams_of[2], (TILES,), jnp.float32) ** levels(streams_of[2], (TILES,), ((0, 8),), -0.2, 0.2)), 0.19921875, 1.0).astype(jnp.bfloat16)
    expert_id_keys = jax.random.split(jax.random.fold_in(streams_of[3], 1), TILES // TILES_DEV)
    expert_id_turns = jax.random.permutation(jax.random.fold_in(streams_of[3], 3), TILES // TILES_DEV)
    expert_id = jax.vmap(lambda own, number: deal_out(jax.random.fold_in(streams_of[3], 2), own, number, TILES_DEV, EXPERTS, 1, CAP, 2))(expert_id_keys, expert_id_turns).reshape((TILES, 1))
    w_conv = gaussian(streams_of[4], (EXPERTS, 3, 3, DG, F), (9 * DG) ** -0.5, 0.375, ((0, 8), (4, 4)))
    w_depth = gaussian(streams_of[5], (EXPERTS, 9, F), 9 ** -0.5, 2.0, ((0, 8), (2, 4)))
    w_out = gaussian(streams_of[6], (EXPERTS, F, D), F ** -0.5, 0.046875, ((0, 8), (1, 4)))
    return {"tiles_in": tiles_in, "grad_out": grad_out, "gate": gate, "expert_id": expert_id, "w_conv": w_conv, "w_depth": w_depth, "w_out": w_out}


def group_conv(field, kernel, count):
    return lax.conv_general_dilated(field, kernel, (1, 1), 'SAME', dimension_numbers=('NHWC', 'HWIO', 'NHWC'), feature_group_count=count, preferred_element_type=jnp.float32)

def conv_back(field, kernel, count, cotangent):
    forward_value, pullback = jax.vjp(lambda value: group_conv(value, kernel, count), field)
    return pullback(cotangent)[0]

def gelu_slope(value):
    normal_cdf = 0.5 * (1.0 + jax.scipy.special.erf(value * 0.7071067811865476))
    return normal_cdf + value * jnp.exp(-0.5 * value * value) * 0.3989422804014327

def depth_forward(field, taps):
    side = field.shape[1]
    padded = jnp.pad(field, ((0, 0), (1, 1), (1, 1), (0, 0))).astype(jnp.float32)
    total = jnp.zeros(field.shape, jnp.float32)
    for row_off in range(3):
        for col_off in range(3):
            total = total + padded[:, row_off:row_off + side, col_off:col_off + side, :] * taps[3 * row_off + col_off].astype(jnp.float32)
    return total

def depth_back(field, taps):
    side = field.shape[1]
    padded = jnp.pad(field, ((0, 0), (1, 1), (1, 1), (0, 0))).astype(jnp.float32)
    total = jnp.zeros(field.shape, jnp.float32)
    for row_off in range(3):
        for col_off in range(3):
            total = total + padded[:, 2 - row_off:2 - row_off + side, 2 - col_off:2 - col_off + side, :] * taps[3 * row_off + col_off].astype(jnp.float32)
    return total

def one_expert(items):
    inputs, grads, gates, kernel, taps, project = items
    slots = inputs.shape[0]
    h_one = group_conv(inputs, kernel, GROUPS)
    active = jax.nn.gelu(h_one, approximate=False).astype(jnp.bfloat16)
    h_two = depth_forward(active, taps).astype(jnp.bfloat16)
    upper = jnp.dot(grads.reshape(-1, D).astype(jnp.float32), project.astype(jnp.float32).T)
    upper = upper.reshape(slots, TS, TS, F)
    gate_grad = lax.optimization_barrier(jnp.sum(h_two.astype(jnp.float32) * upper, axis=(1, 2, 3)))
    d_two = (gates.astype(jnp.float32)[:, None, None, None] * upper).astype(jnp.bfloat16)
    d_act = depth_back(d_two, taps)
    d_one = (d_act * gelu_slope(h_one)).astype(jnp.bfloat16)
    d_input = conv_back(inputs, kernel, GROUPS, d_one.astype(jnp.float32))
    return (d_input.astype(jnp.bfloat16), gate_grad.astype(jnp.bfloat16))

def reference(tiles_in, grad_out, gate, expert_id, w_conv, w_depth, w_out):
    chosen = expert_id[:, 0].astype(jnp.int32)
    matches = (chosen[:, None] == jnp.arange(EXPERTS, dtype=jnp.int32)[None, :]).astype(jnp.int32)
    blocked = matches.reshape(N_EXPERT, TILES_DEV, EXPERTS)
    before = jnp.cumsum(blocked, axis=1) - blocked
    rank = lax.optimization_barrier(jnp.sum(before * blocked, axis=2)).reshape(TILES)
    source = jnp.arange(TILES, dtype=jnp.int32) // TILES_DEV
    slot = (source * CAP + rank).astype(jnp.int32)
    slots = N_EXPERT * CAP
    input_buf = jnp.zeros((EXPERTS, slots, TS, TS, D), jnp.bfloat16).at[chosen, slot].set(tiles_in)
    grad_buf = jnp.zeros((EXPERTS, slots, TS, TS, D), jnp.bfloat16).at[chosen, slot].set(grad_out)
    gate_buf = jnp.zeros((EXPERTS, slots), jnp.bfloat16).at[chosen, slot].set(gate)
    taps = w_depth
    d_buf, g_buf = lax.map(one_expert, (input_buf, grad_buf, gate_buf, w_conv, taps, w_out))
    return (d_buf[chosen, slot], g_buf[chosen, slot])
```

```python
import functools
import jax
import jax.numpy as jnp
import numpy as np
from jax import lax
from jax.experimental import pallas as pl
from jax.experimental.pallas import tpu as pltpu
from jax.sharding import PartitionSpec as P

CAP = 2


def group_conv(field, kernel, count):
    return lax.conv_general_dilated(
        field,
        kernel,
        (1, 1),
        "SAME",
        dimension_numbers=("NHWC", "HWIO", "NHWC"),
        feature_group_count=count,
        preferred_element_type=jnp.float32,
    )


def conv_back(field, kernel, count, cotangent):
    forward_value, pullback = jax.vjp(lambda value: group_conv(value, kernel, count), field)
    return pullback(cotangent)[0]


def gelu_slope(value):
    normal_cdf = 0.5 * (1.0 + jax.scipy.special.erf(value * 0.7071067811865476))
    return normal_cdf + value * jnp.exp(-0.5 * value * value) * 0.3989422804014327


def depth_forward(field, taps):
    side = field.shape[1]
    padded = jnp.pad(field, ((0, 0), (1, 1), (1, 1), (0, 0))).astype(jnp.float32)
    total = jnp.zeros(field.shape, jnp.float32)
    for row_off in range(3):
        for col_off in range(3):
            total = total + padded[:, row_off : row_off + side, col_off : col_off + side, :] * taps[
                3 * row_off + col_off
            ].astype(jnp.float32)
    return total


def depth_back(field, taps):
    side = field.shape[1]
    padded = jnp.pad(field, ((0, 0), (1, 1), (1, 1), (0, 0))).astype(jnp.float32)
    total = jnp.zeros(field.shape, jnp.float32)
    for row_off in range(3):
        for col_off in range(3):
            total = total + padded[
                :, 2 - row_off : 2 - row_off + side, 2 - col_off : 2 - col_off + side, :
            ] * taps[3 * row_off + col_off].astype(jnp.float32)
    return total


def on_device_plain(tiles_in, grad_out, gate, expert_id, w_conv, w_depth, w_out):
    owned, side = (tiles_in.shape[0], tiles_in.shape[1])
    local_feat = tiles_in.shape[3]
    sections = lax.axis_size("expert")
    capacity = CAP
    slots = sections * capacity
    chosen = expert_id[:, 0]
    matches = (chosen[:, None] == jnp.arange(sections, dtype=jnp.int32)[None, :]).astype(jnp.int32)
    rows_idx = jnp.arange(owned, dtype=jnp.int32)
    earlier = (rows_idx[:, None] > rows_idx[None, :]).astype(jnp.int32)
    before = jnp.dot(earlier, matches)
    rank = jnp.sum(before * matches, axis=1)
    slot = chosen * capacity + rank
    placing = (slot[:, None] == jnp.arange(slots, dtype=jnp.int32)[None, :]).astype(jnp.bfloat16)
    flat = jnp.concatenate([tiles_in.reshape(owned, -1), grad_out.reshape(owned, -1)], axis=1)
    outward = lax.dot_general(
        placing, flat, (((0,), (0,)), ((), ())), preferred_element_type=jnp.float32
    ).astype(jnp.bfloat16)
    gate_out = lax.dot_general(
        placing,
        gate.reshape(owned, 1),
        (((0,), (0,)), ((), ())),
        preferred_element_type=jnp.float32,
    ).astype(jnp.bfloat16)
    arrived, gate_in = (
        lax.all_to_all(
            outward.reshape(sections, capacity, -1),
            "expert",
            split_axis=0,
            concat_axis=0,
            tiled=True,
        ),
        lax.all_to_all(
            gate_out.reshape(sections, capacity), "expert", split_axis=0, concat_axis=0, tiled=True
        ),
    )
    width = side * side * local_feat
    arrived = arrived.reshape(slots, 2 * width)
    inputs = arrived[:, :width].reshape(slots, side, side, local_feat)
    grads = arrived[:, width:].reshape(slots, side, side, local_feat)
    gates = gate_in.reshape(slots).astype(jnp.float32)
    kernel = w_conv[0]
    taps = w_depth[0]
    project = w_out[0]
    hidden = project.shape[0]
    count = local_feat // kernel.shape[2]
    h_one = group_conv(inputs, kernel, count)
    active = jax.nn.gelu(h_one, approximate=False).astype(jnp.bfloat16)
    h_two = depth_forward(active, taps).astype(jnp.bfloat16)
    gathered = lax.all_gather(grads, "chan", axis=3, tiled=True)
    upper = lax.dot_general(
        gathered.reshape(slots * side * side, -1),
        project,
        (((1,), (1,)), ((), ())),
        preferred_element_type=jnp.float32,
    )
    upper = upper.reshape(slots, side, side, hidden)
    partial_grad = jnp.sum(h_two.astype(jnp.float32) * upper, axis=(1, 2, 3))
    gate_grad = lax.psum(partial_grad, "chan").astype(jnp.bfloat16)
    d_two = (gates[:, None, None, None] * upper).astype(jnp.bfloat16)
    d_act = depth_back(d_two, taps)
    d_one = (d_act * gelu_slope(h_one)).astype(jnp.bfloat16)
    d_input = conv_back(inputs, kernel, count, d_one.astype(jnp.float32))
    back_rows, back_gate = (
        lax.all_to_all(
            d_input.reshape(sections, capacity, -1),
            "expert",
            split_axis=0,
            concat_axis=0,
            tiled=True,
        ),
        lax.all_to_all(
            gate_grad.reshape(sections, capacity), "expert", split_axis=0, concat_axis=0, tiled=True
        ),
    )
    grad_input = jnp.dot(
        placing, back_rows.reshape(slots, -1), preferred_element_type=jnp.float32
    ).astype(jnp.bfloat16)
    grad_gate = jnp.dot(
        placing, back_gate.reshape(slots, 1), preferred_element_type=jnp.float32
    ).astype(jnp.bfloat16)
    return (grad_input.reshape(owned, side, side, local_feat), grad_gate.reshape(owned))


LANES = 128
GROUP_OUT = 256
MESH = pl.DeviceIdType.MESH


def offsets(side):
    found = []
    for row in range(-1, 2):
        for col in range(-1, 2):
            found.append((row, col))
    return found


def shifted(side, position, row, col):
    at_row, at_col = position // side + row, position % side + col
    if 0 <= at_row < side and 0 <= at_col < side:
        return at_row * side + at_col
    return None


def by_quarter(quarter, parts):
    shape = next(part for part in parts if part is not None).shape
    total = None
    for index, part in enumerate(parts):
        part = jnp.zeros(shape, jnp.float32) if part is None else part
        total = part if total is None else jnp.where(quarter == index, part, total)
    return total


def expert_kernel(
    dims,
    ids_ref,
    x_ref,
    g_ref,
    base_row_ref,
    base_col_ref,
    order_ref,
    order_back_ref,
    taps_ref,
    wc_hbm,
    wo_hbm,
    out_ref,
    wc,
    wo,
    zbuf,
    send,
    recv,
    xbuf,
    gbuf,
    xcol,
    h2,
    slope,
    upper,
    dz,
    gates,
    wc_sem,
    wo_sem,
    zsend_sem,
    zrecv_sem,
    send_sem,
    recv_sem,
    gsend_sem,
    grecv_sem,
):
    n_e, n_c, owned, tiles_t, side = dims
    spots = side * side
    pairs = (spots + 1) // 2
    slots = n_e * CAP
    groups = wc.shape[1] // GROUP_OUT
    per_t = groups // tiles_t
    width = tiles_t * LANES
    piece = 2 * CAP * tiles_t
    me, z = lax.axis_index("expert"), lax.axis_index("chan")
    offs = offsets(side)
    taps_used = len(offs)

    order = []
    for step in range(n_c):
        block = 0
        for at in range(n_c):
            ranked = sorted(range(n_c), key=lambda other: (abs(other - at), other if 2 * at < n_c else -other))
            block = block + jnp.where(z == at, ranked[step], 0)
        order.append(block)

    wc_copy = pltpu.make_async_copy(wc_hbm, wc.at[pl.ds(0, wc_hbm.shape[0])], wc_sem)
    wc_copy.start()
    wo_copies = []
    for step in range(n_c):
        start = pl.multiple_of(order[step] * width, width)
        wo_copies.append(
            pltpu.make_async_copy(wo_hbm.at[:, pl.ds(start, width)], wo.at[step], wo_sem.at[step])
        )
        wo_copies[step].start()

    barrier = pltpu.get_barrier_semaphore()
    for step in range(1, n_e):
        pl.semaphore_signal(
            barrier, inc=1, device_id=(lax.rem(me + step, n_e), z), device_id_type=MESH
        )
    for step in range(1, n_c):
        pl.semaphore_signal(
            barrier, inc=1, device_id=(me, lax.rem(z + step, n_c)), device_id_type=MESH
        )

    names = [ids_ref[tile] for tile in range(owned)]
    codes = []
    for tile in range(owned):
        rank = jnp.int32(0)
        for earlier in range(tile):
            rank = rank + jnp.where(names[earlier] == names[tile], 1, 0)
        codes.append(names[tile] * piece + rank * tiles_t)
    rows_here, rows_routed = 2 * owned * tiles_t, n_e * piece

    def target(base):
        total = base & 0xFFFF
        at_tile = base >> 16
        for tile in range(owned):
            total = total + jnp.where(at_tile == tile, codes[tile], 0)
        return total

    place = jnp.where(
        lax.broadcasted_iota(jnp.int32, (rows_routed, rows_here), 0) == target(base_row_ref[...]),
        1.0,
        0.0,
    ).astype(jnp.bfloat16)

    def route(block, load):
        for pair in range(pairs):
            routed = jnp.dot(place, load(pair), preferred_element_type=jnp.float32)
            send[block, :, pair] = routed.astype(jnp.bfloat16).reshape(n_e, piece, LANES)

    def exchange(block):
        copies = []
        for step in range(1, n_e):
            peer = lax.rem(me + step, n_e)
            copies.append(
                pltpu.make_async_remote_copy(
                    src_ref=send.at[block, peer],
                    dst_ref=recv.at[block, me],
                    send_sem=send_sem.at[block, step],
                    recv_sem=recv_sem.at[block, step],
                    device_id=(peer, z),
                    device_id_type=MESH,
                )
            )
        return copies

    def keep_own(block):
        recv[block, me] = send[block, me]

    def unroute(block, store):
        for pair in range(pairs):
            got = recv[block, :, pair].reshape(rows_routed, LANES)
            got = jnp.dot(order_ref[...], got, preferred_element_type=jnp.float32)
            store(pair, got.astype(jnp.bfloat16).reshape(2, tiles_t, slots, LANES))

    def z_copy(source, block, toward):
        return pltpu.make_async_remote_copy(
            src_ref=source,
            dst_ref=zbuf.at[block],
            send_sem=zsend_sem.at[block, (toward + 1) // 2],
            recv_sem=zrecv_sem.at[block],
            device_id=(me, z + toward),
            device_id_type=MESH,
        )

    x_block = n_c
    back_block = n_c + 1
    route(x_block, lambda pair: x_ref[pair])
    route(0, lambda pair: g_ref[pair])
    keep_own(x_block)
    keep_own(0)
    pl.semaphore_wait(barrier, n_e - 1 + n_c - 1)

    @pl.when(z > 0)
    def _():
        z_copy(g_ref, z, -1).start()

    @pl.when(z < n_c - 1)
    def _():
        z_copy(g_ref, z, 1).start()

    all_copies = {}
    for block in (x_block, 0):
        all_copies[block] = exchange(block)
        for copy in all_copies[block]:
            copy.start()

    def take_z(step):
        block = order[step]
        z_copy(zbuf.at[block], block, 1).wait_recv()

        @pl.when((block < z) & (z < n_c - 1))
        def _():
            z_copy(zbuf.at[block], block, 1).start()

        @pl.when((block > z) & (z > 0))
        def _():
            z_copy(zbuf.at[block], block, -1).start()

        route(step, lambda pair: zbuf[block, pair])
        keep_own(step)
        all_copies[step] = exchange(step)
        for copy in all_copies[step]:
            copy.start()

    quarter = lax.broadcasted_iota(jnp.int32, (slots, LANES), 1) // (LANES // per_t)
    half = LANES // per_t

    def forward(tile_t):
        field = jnp.concatenate([xbuf[tile_t, spot] for spot in range(spots)], axis=0).astype(jnp.float32)
        turned = [field] + [pltpu.roll(field, half * turn, 1) for turn in range(1, per_t)]

        def part(turn, spot):
            return None if spot is None else turned[turn][spot * slots : (spot + 1) * slots]

        for inner in range(per_t):
            for spot in range(spots):
                for lane_tile in range(wc.shape[0] // LANES):
                    parts = []
                    for at in range(per_t):
                        offset = lane_tile * per_t + at
                        source = shifted(side, spot, *offs[offset]) if offset < taps_used else None
                        parts.append(part((at - inner) % per_t, source))
                    if all(item is None for item in parts):
                        value = jnp.zeros((slots, LANES), jnp.float32)
                    else:
                        value = by_quarter(quarter, parts)
                    xcol[
                        inner,
                        spot * slots : (spot + 1) * slots,
                        lane_tile * LANES : (lane_tile + 1) * LANES,
                    ] = value.astype(jnp.bfloat16)

        def each(inner, carry):
            group = tile_t * per_t + inner
            lanes = pl.ds(pl.multiple_of(group * GROUP_OUT, GROUP_OUT), GROUP_OUT)
            h_one = jnp.dot(xcol[inner], wc[:, lanes], preferred_element_type=jnp.float32)
            for cut in range(GROUP_OUT // LANES):
                value = h_one[:, cut * LANES : (cut + 1) * LANES]
                cdf = 0.5 * (1.0 + lax.erf(value * 0.7071067811865476))
                slant = cdf + value * jnp.exp(-0.5 * value * value) * 0.3989422804014327
                slope[group, :, cut * LANES : (cut + 1) * LANES] = slant
                active = (value * cdf).astype(jnp.bfloat16).astype(jnp.float32)
                taps = taps_ref[group, :, cut * LANES : (cut + 1) * LANES].astype(jnp.float32)
                for spot in range(spots):
                    total = None
                    for index, (row, col) in enumerate(offs):
                        source = shifted(side, spot, row, col)
                        if source is not None:
                            term = active[source * slots : (source + 1) * slots] * taps[index : index + 1]
                            total = term if total is None else total + term
                    h2[
                        group, spot * slots : (spot + 1) * slots, cut * LANES : (cut + 1) * LANES
                    ] = total.astype(jnp.bfloat16)
            return carry

        lax.fori_loop(0, per_t, each, 0)

    if n_c > 1:
        take_z(1)
    for copy in all_copies[x_block]:
        copy.wait_recv()

    def store_x(pair, value):
        for parity in range(2):
            for tile_t in range(tiles_t):
                xbuf[tile_t, 2 * pair + parity] = value[parity, tile_t]

    unroute(x_block, store_x)
    wc[pl.ds(wc_hbm.shape[0], wc.shape[0] - wc_hbm.shape[0])] = jnp.zeros(
        (wc.shape[0] - wc_hbm.shape[0], wc.shape[1]), jnp.bfloat16
    )
    wc_copy.wait()
    lax.fori_loop(0, tiles_t // 2, lambda at, carry: (forward(at), carry)[1], 0)
    for step in range(2, min(3, n_c)):
        take_z(step)
    lax.fori_loop(tiles_t // 2, tiles_t, lambda at, carry: (forward(at), carry)[1], 0)
    for step in range(3, n_c):
        take_z(step)

    gate = xbuf[0, spots].astype(jnp.float32)

    def store_g(pair, value):
        for parity in range(2):
            if 2 * pair + parity < spots:
                for tile_t in range(tiles_t):
                    gbuf[
                        (2 * pair + parity) * slots : (2 * pair + parity + 1) * slots,
                        tile_t * LANES : (tile_t + 1) * LANES,
                    ] = value[parity, tile_t]

    gates[z] = jnp.zeros((slots, LANES), jnp.float32)
    for step in range(n_c):
        for copy in all_copies[step]:
            copy.wait_recv()
        unroute(step, store_g)
        wo_copies[step].wait()

        def each(group, carry):
            rows = pl.ds(pl.multiple_of(group * GROUP_OUT, GROUP_OUT), GROUP_OUT)
            product = lax.dot_general(
                gbuf[...], wo[step, rows], (((1,), (1,)), ((), ())), preferred_element_type=jnp.float32
            )
            if step:
                product = product + upper[group]
            upper[group] = product
            if step == n_c - 1:
                both = product * h2[group].astype(jnp.float32)
                for spot in range(spots):
                    for cut in range(GROUP_OUT // LANES):
                        carry = carry + both[
                            spot * slots : (spot + 1) * slots, cut * LANES : (cut + 1) * LANES
                        ]
            return carry

        summed = lax.fori_loop(0, groups, each, jnp.zeros((slots, LANES), jnp.float32))
    gates[z] = summed
    gate_copies = []
    for step in range(1, n_c):
        gate_copies.append(
            pltpu.make_async_remote_copy(
                src_ref=gates.at[z],
                dst_ref=gates.at[z],
                send_sem=gsend_sem.at[step],
                recv_sem=grecv_sem.at[step],
                device_id=(me, lax.rem(z + step, n_c)),
                device_id_type=MESH,
            )
        )
        gate_copies[-1].start()

    def backward(tile_t, carry):
        folded = []
        for inner in range(per_t):
            group = tile_t * per_t + inner
            lanes = pl.ds(pl.multiple_of(group * GROUP_OUT, GROUP_OUT), GROUP_OUT)
            sides = []
            for cut in range(GROUP_OUT // LANES):
                where = slice(cut * LANES, (cut + 1) * LANES)
                taps = taps_ref[group, :, where].astype(jnp.float32)
                d_two = [
                    (gate * upper[group, spot * slots : (spot + 1) * slots, where])
                    .astype(jnp.bfloat16)
                    .astype(jnp.float32)
                    for spot in range(spots)
                ]
                done = []
                for spot in range(spots):
                    total = None
                    for index, (row, col) in enumerate(offs):
                        source = shifted(side, spot, -row, -col)
                        if source is not None:
                            term = d_two[source] * taps[index : index + 1]
                            total = term if total is None else total + term
                    slant = slope[group, spot * slots : (spot + 1) * slots, where]
                    done.append((total * slant).astype(jnp.bfloat16))
                sides.append(jnp.concatenate(done, axis=0))
            d_one = jnp.concatenate(sides, axis=1)
            spread = lax.dot_general(
                d_one, wc[:, lanes], (((1,), (1,)), ((), ())), preferred_element_type=jnp.float32
            )
            sums = []
            for spot in range(spots):
                total = None
                for lane_tile in range(wc.shape[0] // LANES):
                    parts = []
                    for at in range(per_t):
                        offset = lane_tile * per_t + at
                        source = None
                        if offset < taps_used:
                            source = shifted(side, spot, -offs[offset][0], -offs[offset][1])
                        parts.append(
                            None
                            if source is None
                            else spread[
                                source * slots : (source + 1) * slots,
                                lane_tile * LANES : (lane_tile + 1) * LANES,
                            ]
                        )
                    if any(item is not None for item in parts):
                        value = by_quarter(quarter, parts)
                        total = value if total is None else total + value
                sums.append(total)
            folded.append(sums)
        for spot in range(spots):
            total = None
            for turn in range(per_t):
                value = by_quarter(
                    quarter, [folded[(at + turn) % per_t][spot] for at in range(per_t)]
                )
                value = pltpu.roll(value, half * turn, 1) if turn else value
                total = value if total is None else total + value
            dz[spot, tile_t] = total.astype(jnp.bfloat16)
        return carry

    lax.fori_loop(0, tiles_t, backward, 0)
    for copy in gate_copies:
        copy.wait_recv()
    total = gates[0]
    for at in range(1, n_c):
        total = total + gates[at]
    total = jnp.broadcast_to(jnp.sum(total, axis=1, keepdims=True), (slots, LANES))
    for tile_t in range(tiles_t):
        dz[spots, tile_t] = total.astype(jnp.bfloat16)

    for pair in range(pairs):
        field = dz[2 * pair : 2 * pair + 2].reshape(rows_routed, LANES)
        field = jnp.dot(order_back_ref[...], field, preferred_element_type=jnp.float32)
        send[back_block, :, pair] = field.astype(jnp.bfloat16).reshape(n_e, piece, LANES)
    all_copies[back_block] = exchange(back_block)
    for copy in all_copies[back_block]:
        copy.start()
    keep_own(back_block)
    place_back = jnp.where(
        lax.broadcasted_iota(jnp.int32, (rows_here, rows_routed), 1) == target(base_col_ref[...]),
        1.0,
        0.0,
    ).astype(jnp.bfloat16)
    for copy in all_copies[back_block]:
        copy.wait_recv()
    for pair in range(pairs):
        got = recv[back_block, :, pair].reshape(rows_routed, LANES)
        out_ref[pair] = jnp.dot(place_back, got, preferred_element_type=jnp.float32).astype(jnp.bfloat16)

    for block in all_copies:
        for copy in all_copies[block]:
            copy.wait_send()
    for copy in gate_copies:
        copy.wait_send()

    @pl.when(z > 0)
    def _():
        z_copy(g_ref, z, -1).wait_send()

    @pl.when(z < n_c - 1)
    def _():
        z_copy(g_ref, z, 1).wait_send()

    for step in range(1, n_c):
        block = order[step]

        @pl.when((block < z) & (z < n_c - 1))
        def _():
            z_copy(zbuf.at[block], block, 1).wait_send()

        @pl.when((block > z) & (z > 0))
        def _():
            z_copy(zbuf.at[block], block, -1).wait_send()


def on_device(tiles_in, grad_out, gate, expert_id, w_conv, w_depth, w_out):
    owned, side, local_feat = tiles_in.shape[0], tiles_in.shape[1], tiles_in.shape[3]
    n_e, n_c = lax.axis_size("expert"), lax.axis_size("chan")
    hidden = w_out.shape[1]
    tiles_t = local_feat // LANES
    spots = side * side
    pairs = (spots + 1) // 2
    slots = n_e * CAP
    piece = 2 * CAP * tiles_t
    groups = hidden // GROUP_OUT
    group_in = w_conv.shape[3]
    rows_here, rows_routed = 2 * owned * tiles_t, n_e * piece

    def by_spot(field, last):
        field = field.reshape(owned, spots, tiles_t, LANES)
        last = jnp.broadcast_to(last.reshape(owned, 1, 1, 1), (owned, 1, tiles_t, LANES))
        field = jnp.concatenate([field, last], axis=1)
        return field.transpose(1, 0, 2, 3).reshape(pairs, rows_here, LANES)

    x = by_spot(tiles_in, gate)
    g = by_spot(grad_out, jnp.zeros_like(gate))

    column = np.arange(rows_here)
    parity, tile, lane_t = column // (owned * tiles_t), column // tiles_t % owned, column % tiles_t
    base = (tile << 16) + parity * CAP * tiles_t + lane_t
    base_row = jnp.asarray(base.reshape(1, -1), jnp.int32)
    base_col = jnp.asarray(base.reshape(-1, 1), jnp.int32)
    row = np.arange(rows_routed)
    parity, lane_t = row // (tiles_t * slots), row // slots % tiles_t
    source, rank = row % slots // CAP, row % CAP
    order = np.zeros((rows_routed, rows_routed), np.float32)
    order[row, ((source * 2 + parity) * CAP + rank) * tiles_t + lane_t] = 1.0
    taps = w_depth[0].reshape(9, groups, GROUP_OUT).transpose(1, 0, 2)
    taps_rows = 9 * group_in
    padded_rows = -(-taps_rows // LANES) * LANES
    dims = (n_e, n_c, owned, tiles_t, side)
    vmem = pl.BlockSpec(memory_space=pltpu.VMEM)
    anywhere = pl.BlockSpec(memory_space=pl.ANY)
    blocks = n_c + 2
    bf16, f32 = jnp.bfloat16, jnp.float32
    out = pl.pallas_call(
        functools.partial(expert_kernel, dims),
        out_shape=jax.ShapeDtypeStruct((pairs, rows_here, LANES), bf16),
        in_specs=[pl.BlockSpec(memory_space=pltpu.SMEM)] + [vmem] * 7 + [anywhere] * 2,
        out_specs=vmem,
        scratch_shapes=[
            pltpu.VMEM((padded_rows, hidden), bf16),
            pltpu.VMEM((n_c, hidden, local_feat), bf16),
            pltpu.VMEM((n_c, pairs, rows_here, LANES), bf16),
            pltpu.VMEM((blocks, n_e, pairs, piece, LANES), bf16),
            pltpu.VMEM((blocks, n_e, pairs, piece, LANES), bf16),
            pltpu.VMEM((tiles_t, 2 * pairs, slots, LANES), bf16),
            pltpu.VMEM((spots * slots, local_feat), bf16),
            pltpu.VMEM((LANES // group_in, spots * slots, padded_rows), bf16),
            pltpu.VMEM((groups, spots * slots, GROUP_OUT), bf16),
            pltpu.VMEM((groups, spots * slots, GROUP_OUT), f32),
            pltpu.VMEM((groups, spots * slots, GROUP_OUT), f32),
            pltpu.VMEM((2 * pairs, tiles_t, slots, LANES), bf16),
            pltpu.VMEM((n_c, slots, LANES), f32),
            pltpu.SemaphoreType.DMA,
            pltpu.SemaphoreType.DMA((n_c,)),
            pltpu.SemaphoreType.DMA((n_c, 2)),
            pltpu.SemaphoreType.DMA((n_c,)),
            pltpu.SemaphoreType.DMA((blocks, n_e)),
            pltpu.SemaphoreType.DMA((blocks, n_e)),
            pltpu.SemaphoreType.DMA((n_c,)),
            pltpu.SemaphoreType.DMA((n_c,)),
        ],
        compiler_params=pltpu.CompilerParams(
            collective_id=0, has_side_effects=True, vmem_limit_bytes=56 * 1024 * 1024
        ),
    )(
        expert_id.reshape(owned),
        x,
        g,
        base_row,
        base_col,
        jnp.asarray(order, bf16),
        jnp.asarray(order.T, bf16),
        taps,
        w_conv.reshape(taps_rows, hidden),
        w_out.reshape(hidden, w_out.shape[2]),
    )
    field = out.reshape(2 * pairs, owned, local_feat)
    grad_input = field[:spots].transpose(1, 0, 2).reshape(tiles_in.shape)
    return grad_input, field[spots, :, 0]


def choose(tiles_in, grad_out, gate, expert_id, w_conv, w_depth, w_out):
    owned, side, local_feat = tiles_in.shape[0], tiles_in.shape[1], tiles_in.shape[3]
    count = local_feat // w_conv.shape[3]
    whole = local_feat % LANES == 0 and 2 * CAP * (local_feat // LANES) % 16 == 0
    whole = whole and lax.axis_size("expert") * CAP % 16 == 0 and side % 2 == 1
    whole = whole and w_out.shape[1] == count * GROUP_OUT and LANES % w_conv.shape[3] == 0
    body = on_device if whole else on_device_plain
    return body(tiles_in, grad_out, gate, expert_id, w_conv, w_depth, w_out)


def solution(mesh):
    in_specs = (
        P("expert", None, None, "chan"),
        P("expert", None, None, "chan"),
        P("expert"),
        P("expert", None),
        P("expert", None, None, None, "chan"),
        P("expert", None, "chan"),
        P("expert", "chan", None),
    )
    out_specs = (P("expert", None, None, "chan"), P("expert"))
    return jax.shard_map(
        choose, mesh=mesh, in_specs=in_specs, out_specs=out_specs, check_vma=False
    )
```

```python
import functools
import jax
import jax.numpy as jnp
import numpy as np
from jax import lax
from jax.experimental import pallas as pl
from jax.experimental.pallas import tpu as pltpu
from jax.sharding import PartitionSpec as P

CAP = 2


def group_conv(field, kernel, count):
    return lax.conv_general_dilated(
        field,
        kernel,
        (1, 1),
        "SAME",
        dimension_numbers=("NHWC", "HWIO", "NHWC"),
        feature_group_count=count,
        preferred_element_type=jnp.float32,
    )


def conv_back(field, kernel, count, cotangent):
    forward_value, pullback = jax.vjp(lambda value: group_conv(value, kernel, count), field)
    return pullback(cotangent)[0]


def gelu_slope(value):
    normal_cdf = 0.5 * (1.0 + jax.scipy.special.erf(value * 0.7071067811865476))
    return normal_cdf + value * jnp.exp(-0.5 * value * value) * 0.3989422804014327


def depth_forward(field, taps):
    side = field.shape[1]
    padded = jnp.pad(field, ((0, 0), (1, 1), (1, 1), (0, 0))).astype(jnp.float32)
    total = jnp.zeros(field.shape, jnp.float32)
    for row_off in range(3):
        for col_off in range(3):
            total = total + padded[:, row_off : row_off + side, col_off : col_off + side, :] * taps[
                3 * row_off + col_off
            ].astype(jnp.float32)
    return total


def depth_back(field, taps):
    side = field.shape[1]
    padded = jnp.pad(field, ((0, 0), (1, 1), (1, 1), (0, 0))).astype(jnp.float32)
    total = jnp.zeros(field.shape, jnp.float32)
    for row_off in range(3):
        for col_off in range(3):
            total = total + padded[
                :, 2 - row_off : 2 - row_off + side, 2 - col_off : 2 - col_off + side, :
            ] * taps[3 * row_off + col_off].astype(jnp.float32)
    return total


def on_device_plain(tiles_in, grad_out, gate, expert_id, w_conv, w_depth, w_out):
    owned, side = (tiles_in.shape[0], tiles_in.shape[1])
    local_feat = tiles_in.shape[3]
    sections = lax.axis_size("expert")
    capacity = CAP
    slots = sections * capacity
    chosen = expert_id[:, 0]
    matches = (chosen[:, None] == jnp.arange(sections, dtype=jnp.int32)[None, :]).astype(jnp.int32)
    rows_idx = jnp.arange(owned, dtype=jnp.int32)
    earlier = (rows_idx[:, None] > rows_idx[None, :]).astype(jnp.int32)
    before = jnp.dot(earlier, matches)
    rank = jnp.sum(before * matches, axis=1)
    slot = chosen * capacity + rank
    placing = (slot[:, None] == jnp.arange(slots, dtype=jnp.int32)[None, :]).astype(jnp.bfloat16)
    flat = jnp.concatenate([tiles_in.reshape(owned, -1), grad_out.reshape(owned, -1)], axis=1)
    outward = lax.dot_general(
        placing, flat, (((0,), (0,)), ((), ())), preferred_element_type=jnp.float32
    ).astype(jnp.bfloat16)
    gate_out = lax.dot_general(
        placing,
        gate.reshape(owned, 1),
        (((0,), (0,)), ((), ())),
        preferred_element_type=jnp.float32,
    ).astype(jnp.bfloat16)
    arrived, gate_in = (
        lax.all_to_all(
            outward.reshape(sections, capacity, -1),
            "expert",
            split_axis=0,
            concat_axis=0,
            tiled=True,
        ),
        lax.all_to_all(
            gate_out.reshape(sections, capacity), "expert", split_axis=0, concat_axis=0, tiled=True
        ),
    )
    width = side * side * local_feat
    arrived = arrived.reshape(slots, 2 * width)
    inputs = arrived[:, :width].reshape(slots, side, side, local_feat)
    grads = arrived[:, width:].reshape(slots, side, side, local_feat)
    gates = gate_in.reshape(slots).astype(jnp.float32)
    kernel = w_conv[0]
    taps = w_depth[0]
    project = w_out[0]
    hidden = project.shape[0]
    count = local_feat // kernel.shape[2]
    h_one = group_conv(inputs, kernel, count)
    active = jax.nn.gelu(h_one, approximate=False).astype(jnp.bfloat16)
    h_two = depth_forward(active, taps).astype(jnp.bfloat16)
    gathered = lax.all_gather(grads, "chan", axis=3, tiled=True)
    upper = lax.dot_general(
        gathered.reshape(slots * side * side, -1),
        project,
        (((1,), (1,)), ((), ())),
        preferred_element_type=jnp.float32,
    )
    upper = upper.reshape(slots, side, side, hidden)
    partial_grad = jnp.sum(h_two.astype(jnp.float32) * upper, axis=(1, 2, 3))
    gate_grad = lax.psum(partial_grad, "chan").astype(jnp.bfloat16)
    d_two = (gates[:, None, None, None] * upper).astype(jnp.bfloat16)
    d_act = depth_back(d_two, taps)
    d_one = (d_act * gelu_slope(h_one)).astype(jnp.bfloat16)
    d_input = conv_back(inputs, kernel, count, d_one.astype(jnp.float32))
    back_rows, back_gate = (
        lax.all_to_all(
            d_input.reshape(sections, capacity, -1),
            "expert",
            split_axis=0,
            concat_axis=0,
            tiled=True,
        ),
        lax.all_to_all(
            gate_grad.reshape(sections, capacity), "expert", split_axis=0, concat_axis=0, tiled=True
        ),
    )
    grad_input = jnp.dot(
        placing, back_rows.reshape(slots, -1), preferred_element_type=jnp.float32
    ).astype(jnp.bfloat16)
    grad_gate = jnp.dot(
        placing, back_gate.reshape(slots, 1), preferred_element_type=jnp.float32
    ).astype(jnp.bfloat16)
    return (grad_input.reshape(owned, side, side, local_feat), grad_gate.reshape(owned))


LANES = 128
GROUP_OUT = 256
MESH = pl.DeviceIdType.MESH


def offsets(side):
    found = []
    for row in range(-1, 2):
        for col in range(-1, 2):
            found.append((row, col))
    return found


def shifted(side, position, row, col):
    at_row, at_col = position // side + row, position % side + col
    if 0 <= at_row < side and 0 <= at_col < side:
        return at_row * side + at_col
    return None


def by_quarter(quarter, parts):
    shape = next(part for part in parts if part is not None).shape
    total = None
    for index, part in enumerate(parts):
        part = jnp.zeros(shape, jnp.float32) if part is None else part
        total = part if total is None else jnp.where(quarter == index, part, total)
    return total


def expert_kernel(
    dims,
    ids_ref,
    x_ref,
    g_ref,
    gate_ref,
    base_row_ref,
    base_col_ref,
    order_ref,
    order_back_ref,
    taps_ref,
    wc_hbm,
    wo_hbm,
    out_ref,
    gate_out_ref,
    wc,
    wo,
    flat,
    zbuf,
    send,
    recv,
    xbuf,
    gbuf,
    xcol,
    h2,
    slope,
    upper,
    upper_even,
    upper_odd,
    dz,
    gates,
    wc_sem,
    wo_sem,
    zsend_sem,
    zrecv_sem,
    send_sem,
    recv_sem,
    gsend_sem,
    grecv_sem,
):
    n_e, n_c, owned, tiles_t, side = dims
    spots = side * side
    pairs = (spots + 1) // 2
    slots = n_e * CAP
    groups = wc.shape[1] // GROUP_OUT
    per_t = groups // tiles_t
    width = tiles_t * LANES
    piece = 2 * CAP * tiles_t
    me, z = lax.axis_index("expert"), lax.axis_index("chan")
    offs = offsets(side)
    taps_used = len(offs)

    order = []
    for step in range(n_c):
        block = 0
        for at in range(n_c):
            ranked = sorted(range(n_c), key=lambda other: (abs(other - at), other if 2 * at < n_c else -other))
            block = block + jnp.where(z == at, ranked[step], 0)
        order.append(block)

    wc_copy = pltpu.make_async_copy(wc_hbm, wc.at[pl.ds(0, wc_hbm.shape[0])], wc_sem)
    wc_copy.start()
    wo_copies = []
    for step in range(n_c):
        start = pl.multiple_of(order[step] * width, width)
        wo_copies.append(
            pltpu.make_async_copy(wo_hbm.at[:, pl.ds(start, width)], wo.at[step], wo_sem.at[step])
        )
        wo_copies[step].start()

    barrier = pltpu.get_barrier_semaphore()
    for step in range(1, n_e):
        pl.semaphore_signal(
            barrier, inc=1, device_id=(lax.rem(me + step, n_e), z), device_id_type=MESH
        )
    for step in range(1, n_c):
        pl.semaphore_signal(
            barrier, inc=1, device_id=(me, lax.rem(z + step, n_c)), device_id_type=MESH
        )

    wc[pl.ds(wc_hbm.shape[0], wc.shape[0] - wc_hbm.shape[0])] = jnp.zeros(
        (wc.shape[0] - wc_hbm.shape[0], wc.shape[1]), jnp.bfloat16
    )

    names = [ids_ref[tile] for tile in range(owned)]
    codes = []
    for tile in range(owned):
        rank = jnp.int32(0)
        for earlier in range(tile):
            rank = rank + jnp.where(names[earlier] == names[tile], 1, 0)
        codes.append(names[tile] * piece + rank * tiles_t)
    rows_here, rows_routed = 2 * owned * tiles_t, n_e * piece

    def target(base):
        total = base & 0xFFFF
        at_tile = base >> 16
        for tile in range(owned):
            total = total + jnp.where(at_tile == tile, codes[tile], 0)
        return total

    place = jnp.where(
        lax.broadcasted_iota(jnp.int32, (rows_routed, rows_here), 0) == target(base_row_ref[...]),
        1.0,
        0.0,
    ).astype(jnp.bfloat16)

    strip = 2 * owned

    def route(block, field):
        for pair in range(pairs):
            taken = field[pair * strip : (pair + 1) * strip, :]
            taken = jnp.concatenate(
                [taken[:, at * LANES : (at + 1) * LANES] for at in range(tiles_t)], axis=0
            )
            routed = jnp.dot(place, taken, preferred_element_type=jnp.float32)
            send[block, :, pair] = routed.astype(jnp.bfloat16).reshape(n_e, piece, LANES)

    def exchange(block):
        copies = []
        for step in range(1, n_e):
            peer = lax.rem(me + step, n_e)
            copies.append(
                pltpu.make_async_remote_copy(
                    src_ref=send.at[block, peer],
                    dst_ref=recv.at[block, me],
                    send_sem=send_sem.at[block, step],
                    recv_sem=recv_sem.at[block, step],
                    device_id=(peer, z),
                    device_id_type=MESH,
                )
            )
        return copies

    def keep_own(block):
        recv[block, me] = send[block, me]

    def unroute(block, store):
        for pair in range(pairs):
            got = recv[block, :, pair].reshape(rows_routed, LANES)
            got = jnp.dot(order_ref[...], got, preferred_element_type=jnp.float32)
            store(pair, got.astype(jnp.bfloat16).reshape(2, tiles_t, slots, LANES))

    def z_copy(block, toward):
        return pltpu.make_async_remote_copy(
            src_ref=zbuf.at[block],
            dst_ref=zbuf.at[block],
            send_sem=zsend_sem.at[block, (toward + 1) // 2],
            recv_sem=zrecv_sem.at[block],
            device_id=(me, z + toward),
            device_id_type=MESH,
        )

    x_block = n_c
    back_block = n_c + 1
    zbuf[z] = jnp.concatenate(
        [g_ref[...].astype(jnp.float32), jnp.zeros((owned, width), jnp.float32)], axis=0
    ).astype(jnp.bfloat16)
    diagonal = lax.broadcasted_iota(jnp.int32, (owned, owned), 0) == lax.broadcasted_iota(
        jnp.int32, (owned, owned), 1
    )
    spread_gate = jnp.where(diagonal, gate_ref[...].astype(jnp.float32), 0.0)
    spread_gate = jnp.broadcast_to(jnp.sum(spread_gate, axis=1, keepdims=True), (owned, width))
    flat[...] = jnp.concatenate(
        [x_ref[...].astype(jnp.float32), spread_gate], axis=0
    ).astype(jnp.bfloat16)
    route(x_block, flat)
    keep_own(x_block)
    pl.semaphore_wait(barrier, n_e - 1 + n_c - 1)

    @pl.when(z > 0)
    def _():
        z_copy(z, -1).start()

    @pl.when(z < n_c - 1)
    def _():
        z_copy(z, 1).start()

    all_copies = {}
    all_copies[x_block] = exchange(x_block)
    for copy in all_copies[x_block]:
        copy.start()
    route(0, zbuf.at[z])
    keep_own(0)
    all_copies[0] = exchange(0)
    for copy in all_copies[0]:
        copy.start()

    def take_z(step):
        block = order[step]
        z_copy(block, 1).wait_recv()

        @pl.when((block < z) & (z < n_c - 1))
        def _():
            z_copy(block, 1).start()

        @pl.when((block > z) & (z > 0))
        def _():
            z_copy(block, -1).start()

        route(step, zbuf.at[block])
        keep_own(step)
        all_copies[step] = exchange(step)
        for copy in all_copies[step]:
            copy.start()

    def taps_at(group, cut):
        start = pl.multiple_of(group * GROUP_OUT + cut * LANES, LANES)
        return taps_ref[:, pl.ds(start, LANES)].astype(jnp.float32)

    def project(step, group):
        rows = pl.ds(pl.multiple_of(group * GROUP_OUT, GROUP_OUT), GROUP_OUT)
        return lax.dot_general(
            gbuf[step], wo[step, rows], (((1,), (1,)), ((), ())), preferred_element_type=jnp.float32
        )

    def take_block(step):
        for copy in all_copies[step]:
            copy.wait_recv()

        def store(pair, value):
            for parity in range(2):
                spot = 2 * pair + parity
                if spot < spots:
                    for tile_t in range(tiles_t):
                        gbuf[
                            step,
                            spot * slots : (spot + 1) * slots,
                            tile_t * LANES : (tile_t + 1) * LANES,
                        ] = value[parity, tile_t]

        unroute(step, store)
        wo_copies[step].wait()

    quarter = lax.broadcasted_iota(jnp.int32, (slots, LANES), 1) // (LANES // per_t)
    half = LANES // per_t

    def forward(tile_t, first, step):
        field = jnp.concatenate([xbuf[tile_t, spot] for spot in range(spots)], axis=0).astype(jnp.float32)
        turned = [field] + [pltpu.roll(field, half * turn, 1) for turn in range(1, per_t)]

        def part(turn, spot):
            return None if spot is None else turned[turn][spot * slots : (spot + 1) * slots]

        for inner in range(per_t):
            for spot in range(spots):
                for lane_tile in range(wc.shape[0] // LANES):
                    parts = []
                    for at in range(per_t):
                        offset = lane_tile * per_t + at
                        source = shifted(side, spot, *offs[offset]) if offset < taps_used else None
                        parts.append(part((at - inner) % per_t, source))
                    if all(item is None for item in parts):
                        value = jnp.zeros((slots, LANES), jnp.float32)
                    else:
                        value = by_quarter(quarter, parts)
                    xcol[
                        inner,
                        spot * slots : (spot + 1) * slots,
                        lane_tile * LANES : (lane_tile + 1) * LANES,
                    ] = value.astype(jnp.bfloat16)

        def each(inner, carry):
            group = tile_t * per_t + inner
            lanes = pl.ds(pl.multiple_of(group * GROUP_OUT, GROUP_OUT), GROUP_OUT)
            h_one = jnp.dot(xcol[inner], wc[:, lanes], preferred_element_type=jnp.float32)
            if step is not None:
                for part in range(2):
                    ahead = 2 * ((tile_t - first) * per_t + inner) + part
                    if step:
                        upper[ahead] = upper[ahead] + project(step, ahead)
                    else:
                        upper[ahead] = project(step, ahead)
            for cut in range(GROUP_OUT // LANES):
                value = h_one[:, cut * LANES : (cut + 1) * LANES]
                cdf = 0.5 * (1.0 + lax.erf(value * 0.7071067811865476))
                slant = cdf + value * jnp.exp(-0.5 * value * value) * 0.3989422804014327
                slope[group, :, cut * LANES : (cut + 1) * LANES] = slant
                active = (value * cdf).astype(jnp.bfloat16).astype(jnp.float32)
                taps = taps_at(group, cut)
                for spot in range(spots):
                    total = None
                    for index, (row, col) in enumerate(offs):
                        source = shifted(side, spot, row, col)
                        if source is not None:
                            term = active[source * slots : (source + 1) * slots] * taps[index : index + 1]
                            total = term if total is None else total + term
                    h2[
                        group, spot * slots : (spot + 1) * slots, cut * LANES : (cut + 1) * LANES
                    ] = total.astype(jnp.bfloat16)
            return carry

        lax.fori_loop(0, per_t, each, 0)

    if n_c > 1:
        take_z(1)
    for copy in all_copies[x_block]:
        copy.wait_recv()

    def store_x(pair, value):
        for parity in range(2):
            for tile_t in range(tiles_t):
                xbuf[tile_t, 2 * pair + parity] = value[parity, tile_t]

    unroute(x_block, store_x)
    wc_copy.wait()
    early = min(2, n_c - 1)
    middle = tiles_t // 2
    for half_at in range(2):
        step = half_at if half_at < early else None
        first, last = (middle, tiles_t) if half_at else (0, middle)
        if step is not None:
            take_block(step)

        def walk(tile_t, carry):
            forward(tile_t, first, step)
            return carry

        lax.fori_loop(first, last, walk, 0)
        for at in range(2, n_c):
            if (at == 2) == (half_at == 0):
                take_z(at)
    for step in range(early, n_c):
        take_block(step)

    gate = xbuf[0, spots].astype(jnp.float32)
    uppers = (upper_even, upper_odd)

    def finish(tile_t, carry):
        for inner in range(per_t):
            group = tile_t * per_t + inner
            product = None
            for step in range(early, n_c):
                term = project(step, group)
                product = term if product is None else product + term
            if early:
                product = product + upper[group]
            uppers[tile_t % 2][inner] = product
            both = product * h2[group].astype(jnp.float32)
            for spot in range(spots):
                for cut in range(GROUP_OUT // LANES):
                    carry = carry + both[
                        spot * slots : (spot + 1) * slots, cut * LANES : (cut + 1) * LANES
                    ]
        return carry

    def backward(tile_t):
        folded = []
        for inner in range(per_t):
            group = tile_t * per_t + inner
            lanes = pl.ds(pl.multiple_of(group * GROUP_OUT, GROUP_OUT), GROUP_OUT)
            sides = []
            for cut in range(GROUP_OUT // LANES):
                where = slice(cut * LANES, (cut + 1) * LANES)
                taps = taps_at(group, cut)
                d_two = [
                    (gate * uppers[tile_t % 2][inner, spot * slots : (spot + 1) * slots, where])
                    .astype(jnp.bfloat16)
                    .astype(jnp.float32)
                    for spot in range(spots)
                ]
                done = []
                for spot in range(spots):
                    total = None
                    for index, (row, col) in enumerate(offs):
                        source = shifted(side, spot, -row, -col)
                        if source is not None:
                            term = d_two[source] * taps[index : index + 1]
                            total = term if total is None else total + term
                    slant = slope[group, spot * slots : (spot + 1) * slots, where]
                    done.append((total * slant).astype(jnp.bfloat16))
                sides.append(jnp.concatenate(done, axis=0))
            d_one = jnp.concatenate(sides, axis=1)
            spread = lax.dot_general(
                d_one, wc[:, lanes], (((1,), (1,)), ((), ())), preferred_element_type=jnp.float32
            )
            sums = []
            for spot in range(spots):
                total = None
                for lane_tile in range(wc.shape[0] // LANES):
                    parts = []
                    for at in range(per_t):
                        offset = lane_tile * per_t + at
                        source = None
                        if offset < taps_used:
                            source = shifted(side, spot, -offs[offset][0], -offs[offset][1])
                        parts.append(
                            None
                            if source is None
                            else spread[
                                source * slots : (source + 1) * slots,
                                lane_tile * LANES : (lane_tile + 1) * LANES,
                            ]
                        )
                    if any(item is not None for item in parts):
                        value = by_quarter(quarter, parts)
                        total = value if total is None else total + value
                sums.append(total)
            folded.append(sums)
        for spot in range(spots):
            total = None
            for turn in range(per_t):
                value = by_quarter(
                    quarter, [folded[(at + turn) % per_t][spot] for at in range(per_t)]
                )
                value = pltpu.roll(value, half * turn, 1) if turn else value
                total = value if total is None else total + value
            dz[spot, tile_t] = total.astype(jnp.bfloat16)

    summed = finish(0, jnp.zeros((slots, LANES), jnp.float32))
    for tile_t in range(tiles_t - 1):
        summed = finish(tile_t + 1, summed)
        backward(tile_t)
    gates[z] = summed
    gate_copies = []
    for step in range(1, n_c):
        gate_copies.append(
            pltpu.make_async_remote_copy(
                src_ref=gates.at[z],
                dst_ref=gates.at[z],
                send_sem=gsend_sem.at[step],
                recv_sem=grecv_sem.at[step],
                device_id=(me, lax.rem(z + step, n_c)),
                device_id_type=MESH,
            )
        )
        gate_copies[-1].start()

    backward(tiles_t - 1)
    for copy in gate_copies:
        copy.wait_recv()
    total = gates[0]
    for at in range(1, n_c):
        total = total + gates[at]
    total = jnp.broadcast_to(jnp.sum(total, axis=1, keepdims=True), (slots, LANES))
    for tile_t in range(tiles_t):
        dz[spots, tile_t] = total.astype(jnp.bfloat16)

    for pair in range(pairs):
        field = dz[2 * pair : 2 * pair + 2].reshape(rows_routed, LANES)
        field = jnp.dot(order_back_ref[...], field, preferred_element_type=jnp.float32)
        send[back_block, :, pair] = field.astype(jnp.bfloat16).reshape(n_e, piece, LANES)
    all_copies[back_block] = exchange(back_block)
    for copy in all_copies[back_block]:
        copy.start()
    keep_own(back_block)
    place_back = jnp.where(
        lax.broadcasted_iota(jnp.int32, (rows_here, rows_routed), 1) == target(base_col_ref[...]),
        1.0,
        0.0,
    ).astype(jnp.bfloat16)
    for copy in all_copies[back_block]:
        copy.wait_recv()
    back = []
    for pair in range(pairs):
        got = recv[back_block, :, pair].reshape(rows_routed, LANES)
        got = jnp.dot(place_back, got, preferred_element_type=jnp.float32)
        back.append(
            jnp.concatenate([got[at * strip : (at + 1) * strip] for at in range(tiles_t)], axis=1)
        )
    back = jnp.concatenate(back, axis=0)
    gate_rows = back[spots * owned :, :owned]
    gate_out_ref[...] = jnp.sum(
        jnp.where(diagonal, gate_rows, 0.0), axis=0, keepdims=True
    ).astype(jnp.bfloat16)
    out_ref[...] = back[: spots * owned].astype(jnp.bfloat16)

    for block in all_copies:
        for copy in all_copies[block]:
            copy.wait_send()
    for copy in gate_copies:
        copy.wait_send()

    @pl.when(z > 0)
    def _():
        z_copy(z, -1).wait_send()

    @pl.when(z < n_c - 1)
    def _():
        z_copy(z, 1).wait_send()

    for step in range(1, n_c):
        block = order[step]

        @pl.when((block < z) & (z < n_c - 1))
        def _():
            z_copy(block, 1).wait_send()

        @pl.when((block > z) & (z > 0))
        def _():
            z_copy(block, -1).wait_send()


def on_device(tiles_in, grad_out, gate, expert_id, w_conv, w_depth, w_out):
    owned, side, local_feat = tiles_in.shape[0], tiles_in.shape[1], tiles_in.shape[3]
    n_e, n_c = lax.axis_size("expert"), lax.axis_size("chan")
    hidden = w_out.shape[1]
    tiles_t = local_feat // LANES
    spots = side * side
    pairs = (spots + 1) // 2
    slots = n_e * CAP
    piece = 2 * CAP * tiles_t
    groups = hidden // GROUP_OUT
    group_in = w_conv.shape[3]
    rows_here, rows_routed = 2 * owned * tiles_t, n_e * piece

    column = np.arange(rows_here)
    lane_t, parity, tile = column // (2 * owned), column // owned % 2, column % owned
    base = (tile << 16) + parity * CAP * tiles_t + lane_t
    base_row = jnp.asarray(base.reshape(1, -1), jnp.int32)
    base_col = jnp.asarray(base.reshape(-1, 1), jnp.int32)
    row = np.arange(rows_routed)
    parity, lane_t = row // (tiles_t * slots), row // slots % tiles_t
    source, rank = row % slots // CAP, row % CAP
    order = np.zeros((rows_routed, rows_routed), np.float32)
    order[row, ((source * 2 + parity) * CAP + rank) * tiles_t + lane_t] = 1.0
    taps_rows = 9 * group_in
    padded_rows = -(-taps_rows // LANES) * LANES
    dims = (n_e, n_c, owned, tiles_t, side)
    vmem = pl.BlockSpec(memory_space=pltpu.VMEM)
    anywhere = pl.BlockSpec(memory_space=pl.ANY)
    blocks = n_c + 2
    bf16, f32 = jnp.bfloat16, jnp.float32
    grad_input, grad_gate = pl.pallas_call(
        functools.partial(expert_kernel, dims),
        out_shape=(
            jax.ShapeDtypeStruct((spots * owned, local_feat), bf16),
            jax.ShapeDtypeStruct((1, owned), bf16),
        ),
        in_specs=[pl.BlockSpec(memory_space=pltpu.SMEM)] + [vmem] * 8 + [anywhere] * 2,
        out_specs=(vmem, vmem),
        scratch_shapes=[
            pltpu.VMEM((padded_rows, hidden), bf16),
            pltpu.VMEM((n_c, hidden, local_feat), bf16),
            pltpu.VMEM((2 * pairs * owned, local_feat), bf16),
            pltpu.VMEM((n_c, 2 * pairs * owned, local_feat), bf16),
            pltpu.VMEM((blocks, n_e, pairs, piece, LANES), bf16),
            pltpu.VMEM((blocks, n_e, pairs, piece, LANES), bf16),
            pltpu.VMEM((tiles_t, 2 * pairs, slots, LANES), bf16),
            pltpu.VMEM((n_c, spots * slots, local_feat), bf16),
            pltpu.VMEM((LANES // group_in, spots * slots, padded_rows), bf16),
            pltpu.VMEM((groups, spots * slots, GROUP_OUT), bf16),
            pltpu.VMEM((groups, spots * slots, GROUP_OUT), f32),
            pltpu.VMEM((groups, spots * slots, GROUP_OUT), f32),
            pltpu.VMEM((groups // tiles_t, spots * slots, GROUP_OUT), f32),
            pltpu.VMEM((groups // tiles_t, spots * slots, GROUP_OUT), f32),
            pltpu.VMEM((2 * pairs, tiles_t, slots, LANES), bf16),
            pltpu.VMEM((n_c, slots, LANES), f32),
            pltpu.SemaphoreType.DMA,
            pltpu.SemaphoreType.DMA((n_c,)),
            pltpu.SemaphoreType.DMA((n_c, 2)),
            pltpu.SemaphoreType.DMA((n_c,)),
            pltpu.SemaphoreType.DMA((blocks, n_e)),
            pltpu.SemaphoreType.DMA((blocks, n_e)),
            pltpu.SemaphoreType.DMA((n_c,)),
            pltpu.SemaphoreType.DMA((n_c,)),
        ],
        compiler_params=pltpu.CompilerParams(
            collective_id=0, has_side_effects=True, vmem_limit_bytes=56 * 1024 * 1024
        ),
    )(
        expert_id.reshape(owned),
        tiles_in.transpose(1, 2, 0, 3).reshape(spots * owned, local_feat),
        grad_out.transpose(1, 2, 0, 3).reshape(spots * owned, local_feat),
        gate.reshape(1, owned),
        base_row,
        base_col,
        jnp.asarray(order, bf16),
        jnp.asarray(order.T, bf16),
        w_depth.reshape(9, hidden),
        w_conv.reshape(taps_rows, hidden),
        w_out.reshape(hidden, w_out.shape[2]),
    )
    grad_input = grad_input.reshape(side, side, owned, local_feat).transpose(2, 0, 1, 3)
    return grad_input, grad_gate.reshape(owned)


def choose(tiles_in, grad_out, gate, expert_id, w_conv, w_depth, w_out):
    owned, side, local_feat = tiles_in.shape[0], tiles_in.shape[1], tiles_in.shape[3]
    count = local_feat // w_conv.shape[3]
    whole = local_feat % LANES == 0 and 2 * CAP * (local_feat // LANES) % 16 == 0
    whole = whole and lax.axis_size("expert") * CAP % 16 == 0 and side % 2 == 1 and owned % 8 == 0
    whole = whole and w_out.shape[1] == count * GROUP_OUT and LANES % w_conv.shape[3] == 0
    body = on_device if whole else on_device_plain
    return body(tiles_in, grad_out, gate, expert_id, w_conv, w_depth, w_out)


def solution(mesh):
    in_specs = (
        P("expert", None, None, "chan"),
        P("expert", None, None, "chan"),
        P("expert"),
        P("expert", None),
        P("expert", None, None, None, "chan"),
        P("expert", None, "chan"),
        P("expert", "chan", None),
    )
    out_specs = (P("expert", None, None, "chan"), P("expert"))
    return jax.shard_map(
        choose, mesh=mesh, in_specs=in_specs, out_specs=out_specs, check_vma=False
    )
```

```python
import functools
import jax
import jax.numpy as jnp
import numpy as np
from jax import lax
from jax.experimental import pallas as pl
from jax.experimental.pallas import tpu as pltpu
from jax.sharding import PartitionSpec as P

CAP = 2


def group_conv(field, kernel, count):
    return lax.conv_general_dilated(
        field,
        kernel,
        (1, 1),
        "SAME",
        dimension_numbers=("NHWC", "HWIO", "NHWC"),
        feature_group_count=count,
        preferred_element_type=jnp.float32,
    )


def conv_back(field, kernel, count, cotangent):
    forward_value, pullback = jax.vjp(lambda value: group_conv(value, kernel, count), field)
    return pullback(cotangent)[0]


def gelu_slope(value):
    normal_cdf = 0.5 * (1.0 + jax.scipy.special.erf(value * 0.7071067811865476))
    return normal_cdf + value * jnp.exp(-0.5 * value * value) * 0.3989422804014327


def depth_forward(field, taps):
    side = field.shape[1]
    padded = jnp.pad(field, ((0, 0), (1, 1), (1, 1), (0, 0))).astype(jnp.float32)
    total = jnp.zeros(field.shape, jnp.float32)
    for row_off in range(3):
        for col_off in range(3):
            total = total + padded[:, row_off : row_off + side, col_off : col_off + side, :] * taps[
                3 * row_off + col_off
            ].astype(jnp.float32)
    return total


def depth_back(field, taps):
    side = field.shape[1]
    padded = jnp.pad(field, ((0, 0), (1, 1), (1, 1), (0, 0))).astype(jnp.float32)
    total = jnp.zeros(field.shape, jnp.float32)
    for row_off in range(3):
        for col_off in range(3):
            total = total + padded[
                :, 2 - row_off : 2 - row_off + side, 2 - col_off : 2 - col_off + side, :
            ] * taps[3 * row_off + col_off].astype(jnp.float32)
    return total


def on_device_plain(tiles_in, grad_out, gate, expert_id, w_conv, w_depth, w_out):
    owned, side = (tiles_in.shape[0], tiles_in.shape[1])
    local_feat = tiles_in.shape[3]
    sections = lax.axis_size("expert")
    capacity = CAP
    slots = sections * capacity
    chosen = expert_id[:, 0]
    matches = (chosen[:, None] == jnp.arange(sections, dtype=jnp.int32)[None, :]).astype(jnp.int32)
    rows_idx = jnp.arange(owned, dtype=jnp.int32)
    earlier = (rows_idx[:, None] > rows_idx[None, :]).astype(jnp.int32)
    before = jnp.dot(earlier, matches)
    rank = jnp.sum(before * matches, axis=1)
    slot = chosen * capacity + rank
    placing = (slot[:, None] == jnp.arange(slots, dtype=jnp.int32)[None, :]).astype(jnp.bfloat16)
    flat = jnp.concatenate([tiles_in.reshape(owned, -1), grad_out.reshape(owned, -1)], axis=1)
    outward = lax.dot_general(
        placing, flat, (((0,), (0,)), ((), ())), preferred_element_type=jnp.float32
    ).astype(jnp.bfloat16)
    gate_out = lax.dot_general(
        placing,
        gate.reshape(owned, 1),
        (((0,), (0,)), ((), ())),
        preferred_element_type=jnp.float32,
    ).astype(jnp.bfloat16)
    arrived, gate_in = (
        lax.all_to_all(
            outward.reshape(sections, capacity, -1),
            "expert",
            split_axis=0,
            concat_axis=0,
            tiled=True,
        ),
        lax.all_to_all(
            gate_out.reshape(sections, capacity), "expert", split_axis=0, concat_axis=0, tiled=True
        ),
    )
    width = side * side * local_feat
    arrived = arrived.reshape(slots, 2 * width)
    inputs = arrived[:, :width].reshape(slots, side, side, local_feat)
    grads = arrived[:, width:].reshape(slots, side, side, local_feat)
    gates = gate_in.reshape(slots).astype(jnp.float32)
    kernel = w_conv[0]
    taps = w_depth[0]
    project = w_out[0]
    hidden = project.shape[0]
    count = local_feat // kernel.shape[2]
    h_one = group_conv(inputs, kernel, count)
    active = jax.nn.gelu(h_one, approximate=False).astype(jnp.bfloat16)
    h_two = depth_forward(active, taps).astype(jnp.bfloat16)
    gathered = lax.all_gather(grads, "chan", axis=3, tiled=True)
    upper = lax.dot_general(
        gathered.reshape(slots * side * side, -1),
        project,
        (((1,), (1,)), ((), ())),
        preferred_element_type=jnp.float32,
    )
    upper = upper.reshape(slots, side, side, hidden)
    partial_grad = jnp.sum(h_two.astype(jnp.float32) * upper, axis=(1, 2, 3))
    gate_grad = lax.psum(partial_grad, "chan").astype(jnp.bfloat16)
    d_two = (gates[:, None, None, None] * upper).astype(jnp.bfloat16)
    d_act = depth_back(d_two, taps)
    d_one = (d_act * gelu_slope(h_one)).astype(jnp.bfloat16)
    d_input = conv_back(inputs, kernel, count, d_one.astype(jnp.float32))
    back_rows, back_gate = (
        lax.all_to_all(
            d_input.reshape(sections, capacity, -1),
            "expert",
            split_axis=0,
            concat_axis=0,
            tiled=True,
        ),
        lax.all_to_all(
            gate_grad.reshape(sections, capacity), "expert", split_axis=0, concat_axis=0, tiled=True
        ),
    )
    grad_input = jnp.dot(
        placing, back_rows.reshape(slots, -1), preferred_element_type=jnp.float32
    ).astype(jnp.bfloat16)
    grad_gate = jnp.dot(
        placing, back_gate.reshape(slots, 1), preferred_element_type=jnp.float32
    ).astype(jnp.bfloat16)
    return (grad_input.reshape(owned, side, side, local_feat), grad_gate.reshape(owned))


LANES = 128
GROUP_OUT = 256
MESH = pl.DeviceIdType.MESH


def offsets(side):
    found = []
    for row in range(-1, 2):
        for col in range(-1, 2):
            found.append((row, col))
    return found


def shifted(side, position, row, col):
    at_row, at_col = position // side + row, position % side + col
    if 0 <= at_row < side and 0 <= at_col < side:
        return at_row * side + at_col
    return None


def by_quarter(quarter, parts):
    shape = next(part for part in parts if part is not None).shape
    total = None
    for index, part in enumerate(parts):
        part = jnp.zeros(shape, jnp.float32) if part is None else part
        total = part if total is None else jnp.where(quarter == index, part, total)
    return total


def slot_codes(ids_ref, owned, piece, tiles_t):
    names = [ids_ref[tile] for tile in range(owned)]
    codes = []
    for tile in range(owned):
        rank = jnp.int32(0)
        for earlier in range(tile):
            rank = rank + jnp.where(names[earlier] == names[tile], 1, 0)
        codes.append(names[tile] * piece + rank * tiles_t)
    return codes


def target(base, codes):
    total = base & 0xFFFF
    at_tile = base >> 16
    for tile, code in enumerate(codes):
        total = total + jnp.where(at_tile == tile, code, 0)
    return total


def owner_kernel(dims, ids_ref, base_col_ref, back_ref, out_ref, gate_out_ref):
    n_e, n_c, owned, tiles_t, side = dims
    spots = side * side
    pairs = (spots + 1) // 2
    piece = 2 * CAP * tiles_t
    strip = 2 * owned
    rows_here, rows_routed = 2 * owned * tiles_t, n_e * piece
    codes = slot_codes(ids_ref, owned, piece, tiles_t)
    place_back = jnp.where(
        lax.broadcasted_iota(jnp.int32, (rows_here, rows_routed), 1)
        == target(base_col_ref[...], codes),
        1.0,
        0.0,
    ).astype(jnp.bfloat16)
    for pair in range(pairs):
        got = back_ref[:, pair].reshape(rows_routed, LANES)
        got = jnp.dot(place_back, got, preferred_element_type=jnp.float32)
        got = jnp.concatenate([got[at * strip : (at + 1) * strip] for at in range(tiles_t)], axis=1)
        if pair < pairs - 1:
            out_ref[pair * strip : (pair + 1) * strip] = got.astype(jnp.bfloat16)
        else:
            out_ref[pair * strip :] = got[:owned].astype(jnp.bfloat16)
            rows = got[owned:, :owned]
    diagonal = lax.broadcasted_iota(jnp.int32, (owned, owned), 0) == lax.broadcasted_iota(
        jnp.int32, (owned, owned), 1
    )
    gate_row = jnp.sum(jnp.where(diagonal, rows, 0.0), axis=0, keepdims=True)
    gate_out_ref[...] = gate_row.astype(jnp.bfloat16).reshape(gate_out_ref.shape)


def expert_kernel(
    dims,
    ids_ref,
    x_ref,
    g_ref,
    gate_ref,
    base_row_ref,
    order_ref,
    order_back_ref,
    taps_ref,
    wc_hbm,
    wo_hbm,
    back_ref,
    wc,
    wo,
    flat,
    zbuf,
    send,
    recv,
    xbuf,
    gbuf,
    xcol,
    h2,
    slope,
    partial_first,
    partial_second,
    upper_even,
    upper_odd,
    dz,
    gates,
    wc_sem,
    wo_sem,
    zsend_sem,
    zrecv_sem,
    send_sem,
    recv_sem,
    gsend_sem,
    grecv_sem,
    own_sem,
):
    n_e, n_c, owned, tiles_t, side = dims
    spots = side * side
    pairs = (spots + 1) // 2
    slots = n_e * CAP
    groups = wc.shape[1] // GROUP_OUT
    per_t = groups // tiles_t
    width = tiles_t * LANES
    piece = 2 * CAP * tiles_t
    me, z = lax.axis_index("expert"), lax.axis_index("chan")
    partial = (partial_first, partial_second)
    offs = offsets(side)
    taps_used = len(offs)

    order = []
    for step in range(n_c):
        block = 0
        for at in range(n_c):
            ranked = sorted(range(n_c), key=lambda other: (abs(other - at), other if 2 * at < n_c else -other))
            block = block + jnp.where(z == at, ranked[step], 0)
        order.append(block)

    wc_copy = pltpu.make_async_copy(wc_hbm, wc.at[pl.ds(0, wc_hbm.shape[0])], wc_sem)
    wc_copy.start()
    wo_copies = []
    for step in range(n_c):
        start = pl.multiple_of(order[step] * width, width)
        wo_copies.append(
            pltpu.make_async_copy(wo_hbm.at[:, pl.ds(start, width)], wo.at[step], wo_sem.at[step])
        )
        wo_copies[step].start()

    barrier = pltpu.get_barrier_semaphore()
    for step in range(1, n_e):
        pl.semaphore_signal(
            barrier, inc=1, device_id=(lax.rem(me + step, n_e), z), device_id_type=MESH
        )
    for step in range(1, n_c):
        pl.semaphore_signal(
            barrier, inc=1, device_id=(me, lax.rem(z + step, n_c)), device_id_type=MESH
        )

    wc[pl.ds(wc_hbm.shape[0], wc.shape[0] - wc_hbm.shape[0])] = jnp.zeros(
        (wc.shape[0] - wc_hbm.shape[0], wc.shape[1]), jnp.bfloat16
    )

    codes = slot_codes(ids_ref, owned, piece, tiles_t)
    rows_here, rows_routed = 2 * owned * tiles_t, n_e * piece

    place = jnp.where(
        lax.broadcasted_iota(jnp.int32, (rows_routed, rows_here), 0) == target(base_row_ref[...], codes),
        1.0,
        0.0,
    ).astype(jnp.bfloat16)

    strip = 2 * owned

    def route(block, field):
        for pair in range(pairs):
            taken = field[pair * strip : (pair + 1) * strip, :]
            taken = jnp.concatenate(
                [taken[:, at * LANES : (at + 1) * LANES] for at in range(tiles_t)], axis=0
            )
            routed = jnp.dot(place, taken, preferred_element_type=jnp.float32)
            send[block, :, pair] = routed.astype(jnp.bfloat16).reshape(n_e, piece, LANES)

    def exchange(block):
        copies = []
        for step in range(1, n_e):
            peer = lax.rem(me + step, n_e)
            copies.append(
                pltpu.make_async_remote_copy(
                    src_ref=send.at[block, peer],
                    dst_ref=back_ref.at[me] if block == back_block else recv.at[block, me],
                    send_sem=send_sem.at[block, step],
                    recv_sem=recv_sem.at[block, step],
                    device_id=(peer, z),
                    device_id_type=MESH,
                )
            )
        return copies

    def keep_own(block):
        recv[block, me] = send[block, me]

    def unroute(block, store):
        for pair in range(pairs):
            got = recv[block, :, pair].reshape(rows_routed, LANES)
            got = jnp.dot(order_ref[...], got, preferred_element_type=jnp.float32)
            store(pair, got.astype(jnp.bfloat16).reshape(2, tiles_t, slots, LANES))

    def z_copy(block, toward):
        return pltpu.make_async_remote_copy(
            src_ref=zbuf.at[block],
            dst_ref=zbuf.at[block],
            send_sem=zsend_sem.at[block, (toward + 1) // 2],
            recv_sem=zrecv_sem.at[block],
            device_id=(me, z + toward),
            device_id_type=MESH,
        )

    x_block = n_c
    back_block = n_c + 1
    zbuf[z] = jnp.concatenate(
        [g_ref[...].astype(jnp.float32), jnp.zeros((owned, width), jnp.float32)], axis=0
    ).astype(jnp.bfloat16)
    diagonal = lax.broadcasted_iota(jnp.int32, (owned, owned), 0) == lax.broadcasted_iota(
        jnp.int32, (owned, owned), 1
    )
    spread_gate = jnp.where(diagonal, gate_ref[...].astype(jnp.float32), 0.0)
    spread_gate = jnp.broadcast_to(jnp.sum(spread_gate, axis=1, keepdims=True), (owned, width))
    flat[...] = jnp.concatenate(
        [x_ref[...].astype(jnp.float32), spread_gate], axis=0
    ).astype(jnp.bfloat16)
    route(x_block, flat)
    keep_own(x_block)
    pl.semaphore_wait(barrier, n_e - 1 + n_c - 1)

    @pl.when(z > 0)
    def _():
        z_copy(z, -1).start()

    @pl.when(z < n_c - 1)
    def _():
        z_copy(z, 1).start()

    all_copies = {}
    all_copies[x_block] = exchange(x_block)
    for copy in all_copies[x_block]:
        copy.start()
    route(0, zbuf.at[z])
    keep_own(0)
    all_copies[0] = exchange(0)
    for copy in all_copies[0]:
        copy.start()

    def take_z(step):
        block = order[step]
        z_copy(block, 1).wait_recv()

        @pl.when((block < z) & (z < n_c - 1))
        def _():
            z_copy(block, 1).start()

        @pl.when((block > z) & (z > 0))
        def _():
            z_copy(block, -1).start()

        route(step, zbuf.at[block])
        keep_own(step)
        all_copies[step] = exchange(step)
        for copy in all_copies[step]:
            copy.start()

    def taps_at(group, cut):
        start = pl.multiple_of(group * GROUP_OUT + cut * LANES, LANES)
        return taps_ref[:, pl.ds(start, LANES)].astype(jnp.float32)

    def project(step, group):
        rows = pl.ds(pl.multiple_of(group * GROUP_OUT, GROUP_OUT), GROUP_OUT)
        return lax.dot_general(
            gbuf[step], wo[step, rows], (((1,), (1,)), ((), ())), preferred_element_type=jnp.float32
        )

    def take_block(step):
        for copy in all_copies[step]:
            copy.wait_recv()

        def store(pair, value):
            for parity in range(2):
                spot = 2 * pair + parity
                if spot < spots:
                    for tile_t in range(tiles_t):
                        gbuf[
                            step,
                            spot * slots : (spot + 1) * slots,
                            tile_t * LANES : (tile_t + 1) * LANES,
                        ] = value[parity, tile_t]

        unroute(step, store)
        wo_copies[step].wait()

    quarter = lax.broadcasted_iota(jnp.int32, (slots, LANES), 1) // (LANES // per_t)
    half = LANES // per_t

    def forward(tile_t, first, step):
        field = jnp.concatenate([xbuf[tile_t, spot] for spot in range(spots)], axis=0).astype(jnp.float32)
        turned = [field] + [pltpu.roll(field, half * turn, 1) for turn in range(1, per_t)]

        def part(turn, spot):
            return None if spot is None else turned[turn][spot * slots : (spot + 1) * slots]

        for inner in range(per_t):
            for spot in range(spots):
                for lane_tile in range(wc.shape[0] // LANES):
                    parts = []
                    for at in range(per_t):
                        offset = lane_tile * per_t + at
                        source = shifted(side, spot, *offs[offset]) if offset < taps_used else None
                        parts.append(part((at - inner) % per_t, source))
                    if all(item is None for item in parts):
                        value = jnp.zeros((slots, LANES), jnp.float32)
                    else:
                        value = by_quarter(quarter, parts)
                    xcol[
                        inner,
                        spot * slots : (spot + 1) * slots,
                        lane_tile * LANES : (lane_tile + 1) * LANES,
                    ] = value.astype(jnp.bfloat16)

        def each(inner, carry):
            group = tile_t * per_t + inner
            lanes = pl.ds(pl.multiple_of(group * GROUP_OUT, GROUP_OUT), GROUP_OUT)
            h_one = jnp.dot(xcol[inner], wc[:, lanes], preferred_element_type=jnp.float32)
            if step is not None:
                for part in range(2):
                    ahead = 2 * ((tile_t - first) * per_t + inner) + part
                    partial[step][ahead] = project(step, ahead)
            for cut in range(GROUP_OUT // LANES):
                value = h_one[:, cut * LANES : (cut + 1) * LANES]
                cdf = 0.5 * (1.0 + lax.erf(value * 0.7071067811865476))
                slant = cdf + value * jnp.exp(-0.5 * value * value) * 0.3989422804014327
                slope[group, :, cut * LANES : (cut + 1) * LANES] = slant
                active = (value * cdf).astype(jnp.bfloat16).astype(jnp.float32)
                taps = taps_at(group, cut)
                for spot in range(spots):
                    total = None
                    for index, (row, col) in enumerate(offs):
                        source = shifted(side, spot, row, col)
                        if source is not None:
                            term = active[source * slots : (source + 1) * slots] * taps[index : index + 1]
                            total = term if total is None else total + term
                    h2[
                        group, spot * slots : (spot + 1) * slots, cut * LANES : (cut + 1) * LANES
                    ] = total.astype(jnp.bfloat16)
            return carry

        for inner in range(per_t):
            each(inner, 0)

    if n_c > 1:
        take_z(1)
    for copy in all_copies[x_block]:
        copy.wait_recv()

    def store_x(pair, value):
        for parity in range(2):
            for tile_t in range(tiles_t):
                xbuf[tile_t, 2 * pair + parity] = value[parity, tile_t]

    unroute(x_block, store_x)
    wc_copy.wait()
    early = min(2, n_c - 1)
    middle = tiles_t // 2
    for half_at in range(2):
        step = half_at if half_at < early else None
        first, last = (middle, tiles_t) if half_at else (0, middle)
        if step is not None:
            take_block(step)

        def walk(tile_t, carry):
            forward(tile_t, first, step)
            return carry

        if half_at:
            lax.fori_loop(first, last, walk, 0)
        else:
            for tile_t in range(first, last):
                walk(tile_t, 0)
                for at in range(2, n_c):
                    if at - 2 == tile_t or (tile_t == last - 1 and at - 2 > tile_t):
                        take_z(at)
    for step in range(early, n_c):
        take_block(step)

    gate = xbuf[0, spots].astype(jnp.float32)
    uppers = (upper_even, upper_odd)

    def finish(tile_t, carry):
        for inner in range(per_t):
            group = tile_t * per_t + inner
            product = None
            for step in range(early, n_c):
                term = project(step, group)
                product = term if product is None else product + term
            for step in range(early):
                product = product + partial[step][group]
            uppers[tile_t % 2][inner] = product
            both = product * h2[group].astype(jnp.float32)
            for spot in range(spots):
                for cut in range(GROUP_OUT // LANES):
                    carry = carry + both[
                        spot * slots : (spot + 1) * slots, cut * LANES : (cut + 1) * LANES
                    ]
        return carry

    def backward(tile_t):
        folded = []
        for inner in range(per_t):
            group = tile_t * per_t + inner
            lanes = pl.ds(pl.multiple_of(group * GROUP_OUT, GROUP_OUT), GROUP_OUT)
            sides = []
            for cut in range(GROUP_OUT // LANES):
                where = slice(cut * LANES, (cut + 1) * LANES)
                taps = taps_at(group, cut)
                d_two = [
                    (gate * uppers[tile_t % 2][inner, spot * slots : (spot + 1) * slots, where])
                    .astype(jnp.bfloat16)
                    .astype(jnp.float32)
                    for spot in range(spots)
                ]
                done = []
                for spot in range(spots):
                    total = None
                    for index, (row, col) in enumerate(offs):
                        source = shifted(side, spot, -row, -col)
                        if source is not None:
                            term = d_two[source] * taps[index : index + 1]
                            total = term if total is None else total + term
                    slant = slope[group, spot * slots : (spot + 1) * slots, where]
                    done.append((total * slant).astype(jnp.bfloat16))
                sides.append(jnp.concatenate(done, axis=0))
            d_one = jnp.concatenate(sides, axis=1)
            spread = lax.dot_general(
                d_one, wc[:, lanes], (((1,), (1,)), ((), ())), preferred_element_type=jnp.float32
            )
            sums = []
            for spot in range(spots):
                total = None
                for lane_tile in range(wc.shape[0] // LANES):
                    parts = []
                    for at in range(per_t):
                        offset = lane_tile * per_t + at
                        source = None
                        if offset < taps_used:
                            source = shifted(side, spot, -offs[offset][0], -offs[offset][1])
                        parts.append(
                            None
                            if source is None
                            else spread[
                                source * slots : (source + 1) * slots,
                                lane_tile * LANES : (lane_tile + 1) * LANES,
                            ]
                        )
                    if any(item is not None for item in parts):
                        value = by_quarter(quarter, parts)
                        total = value if total is None else total + value
                sums.append(total)
            folded.append(sums)
        for spot in range(spots):
            total = None
            for turn in range(per_t):
                value = by_quarter(
                    quarter, [folded[(at + turn) % per_t][spot] for at in range(per_t)]
                )
                value = pltpu.roll(value, half * turn, 1) if turn else value
                total = value if total is None else total + value
            dz[spot, tile_t] = total.astype(jnp.bfloat16)

    summed = finish(0, jnp.zeros((slots, LANES), jnp.float32))
    for tile_t in range(tiles_t - 1):
        summed = finish(tile_t + 1, summed)
        backward(tile_t)
    gates[z] = summed
    gate_copies = []
    for step in range(1, n_c):
        gate_copies.append(
            pltpu.make_async_remote_copy(
                src_ref=gates.at[z],
                dst_ref=gates.at[z],
                send_sem=gsend_sem.at[step],
                recv_sem=grecv_sem.at[step],
                device_id=(me, lax.rem(z + step, n_c)),
                device_id_type=MESH,
            )
        )
        gate_copies[-1].start()

    backward(tiles_t - 1)
    for copy in gate_copies:
        copy.wait_recv()
    total = gates[0]
    for at in range(1, n_c):
        total = total + gates[at]
    total = jnp.broadcast_to(jnp.sum(total, axis=1, keepdims=True), (slots, LANES))
    for tile_t in range(tiles_t):
        dz[spots, tile_t] = total.astype(jnp.bfloat16)

    for pair in range(pairs):
        field = dz[2 * pair : 2 * pair + 2].reshape(rows_routed, LANES)
        field = jnp.dot(order_back_ref[...], field, preferred_element_type=jnp.float32)
        send[back_block, :, pair] = field.astype(jnp.bfloat16).reshape(n_e, piece, LANES)
    all_copies[back_block] = exchange(back_block)
    for copy in all_copies[back_block]:
        copy.start()
    own_copy = pltpu.make_async_copy(send.at[back_block, me], back_ref.at[me], own_sem)
    own_copy.start()
    for copy in all_copies[back_block]:
        copy.wait_recv()
    own_copy.wait()

    for block in all_copies:
        for copy in all_copies[block]:
            copy.wait_send()
    for copy in gate_copies:
        copy.wait_send()

    @pl.when(z > 0)
    def _():
        z_copy(z, -1).wait_send()

    @pl.when(z < n_c - 1)
    def _():
        z_copy(z, 1).wait_send()

    for step in range(1, n_c):
        block = order[step]

        @pl.when((block < z) & (z < n_c - 1))
        def _():
            z_copy(block, 1).wait_send()

        @pl.when((block > z) & (z > 0))
        def _():
            z_copy(block, -1).wait_send()


def on_device(tiles_in, grad_out, gate, expert_id, w_conv, w_depth, w_out):
    owned, side, local_feat = tiles_in.shape[0], tiles_in.shape[1], tiles_in.shape[3]
    n_e, n_c = lax.axis_size("expert"), lax.axis_size("chan")
    hidden = w_out.shape[1]
    tiles_t = local_feat // LANES
    spots = side * side
    pairs = (spots + 1) // 2
    slots = n_e * CAP
    piece = 2 * CAP * tiles_t
    groups = hidden // GROUP_OUT
    group_in = w_conv.shape[3]
    rows_here, rows_routed = 2 * owned * tiles_t, n_e * piece

    column = np.arange(rows_here)
    lane_t, parity, tile = column // (2 * owned), column // owned % 2, column % owned
    base = (tile << 16) + parity * CAP * tiles_t + lane_t
    base_row = jnp.asarray(base.reshape(1, -1), jnp.int32)
    base_col = jnp.asarray(base.reshape(-1, 1), jnp.int32)
    row = np.arange(rows_routed)
    parity, lane_t = row // (tiles_t * slots), row // slots % tiles_t
    source, rank = row % slots // CAP, row % CAP
    order = np.zeros((rows_routed, rows_routed), np.float32)
    order[row, ((source * 2 + parity) * CAP + rank) * tiles_t + lane_t] = 1.0
    taps_rows = 9 * group_in
    padded_rows = -(-taps_rows // LANES) * LANES
    dims = (n_e, n_c, owned, tiles_t, side)
    vmem = pl.BlockSpec(memory_space=pltpu.VMEM)
    anywhere = pl.BlockSpec(memory_space=pl.ANY)
    blocks = n_c + 2
    bf16, f32 = jnp.bfloat16, jnp.float32
    ids = expert_id.reshape(owned)
    back = pl.pallas_call(
        functools.partial(expert_kernel, dims),
        out_shape=jax.ShapeDtypeStruct((n_e, pairs, piece, LANES), bf16),
        in_specs=[pl.BlockSpec(memory_space=pltpu.SMEM)] + [vmem] * 7 + [anywhere] * 2,
        out_specs=anywhere,
        scratch_shapes=[
            pltpu.VMEM((padded_rows, hidden), bf16),
            pltpu.VMEM((n_c, hidden, local_feat), bf16),
            pltpu.VMEM((2 * pairs * owned, local_feat), bf16),
            pltpu.VMEM((n_c, 2 * pairs * owned, local_feat), bf16),
            pltpu.VMEM((blocks, n_e, pairs, piece, LANES), bf16),
            pltpu.VMEM((blocks - 1, n_e, pairs, piece, LANES), bf16),
            pltpu.VMEM((tiles_t, 2 * pairs, slots, LANES), bf16),
            pltpu.VMEM((n_c, spots * slots, local_feat), bf16),
            pltpu.VMEM((LANES // group_in, spots * slots, padded_rows), bf16),
            pltpu.VMEM((groups, spots * slots, GROUP_OUT), bf16),
            pltpu.VMEM((groups, spots * slots, GROUP_OUT), f32),
            pltpu.VMEM((groups, spots * slots, GROUP_OUT), f32),
            pltpu.VMEM((groups, spots * slots, GROUP_OUT), f32),
            pltpu.VMEM((groups // tiles_t, spots * slots, GROUP_OUT), f32),
            pltpu.VMEM((groups // tiles_t, spots * slots, GROUP_OUT), f32),
            pltpu.VMEM((2 * pairs, tiles_t, slots, LANES), bf16),
            pltpu.VMEM((n_c, slots, LANES), f32),
            pltpu.SemaphoreType.DMA,
            pltpu.SemaphoreType.DMA((n_c,)),
            pltpu.SemaphoreType.DMA((n_c, 2)),
            pltpu.SemaphoreType.DMA((n_c,)),
            pltpu.SemaphoreType.DMA((blocks, n_e)),
            pltpu.SemaphoreType.DMA((blocks, n_e)),
            pltpu.SemaphoreType.DMA((n_c,)),
            pltpu.SemaphoreType.DMA((n_c,)),
            pltpu.SemaphoreType.DMA,
        ],
        compiler_params=pltpu.CompilerParams(
            collective_id=0, has_side_effects=True, vmem_limit_bytes=56 * 1024 * 1024
        ),
    )(
        ids,
        tiles_in.transpose(1, 2, 0, 3).reshape(spots * owned, local_feat),
        grad_out.transpose(1, 2, 0, 3).reshape(spots * owned, local_feat),
        gate.reshape(1, owned),
        base_row,
        jnp.asarray(order, bf16),
        jnp.asarray(order.T, bf16),
        w_depth.reshape(9, hidden),
        w_conv.reshape(taps_rows, hidden),
        w_out.reshape(hidden, w_out.shape[2]),
    )
    grad_input, grad_gate = pl.pallas_call(
        functools.partial(owner_kernel, dims),
        out_shape=(
            jax.ShapeDtypeStruct((spots * owned, local_feat), bf16),
            jax.ShapeDtypeStruct((owned,), bf16),
        ),
        in_specs=[pl.BlockSpec(memory_space=pltpu.SMEM), vmem, vmem],
        out_specs=(vmem, vmem),
    )(ids, base_col, back)
    grad_input = grad_input.reshape(side, side, owned, local_feat).transpose(2, 0, 1, 3)
    return grad_input, grad_gate


def choose(tiles_in, grad_out, gate, expert_id, w_conv, w_depth, w_out):
    owned, side, local_feat = tiles_in.shape[0], tiles_in.shape[1], tiles_in.shape[3]
    count = local_feat // w_conv.shape[3]
    whole = local_feat % LANES == 0 and 2 * CAP * (local_feat // LANES) % 16 == 0
    whole = whole and lax.axis_size("expert") * CAP % 16 == 0 and side % 2 == 1 and owned % 8 == 0
    whole = whole and w_out.shape[1] == count * GROUP_OUT and LANES % w_conv.shape[3] == 0
    body = on_device if whole else on_device_plain
    return body(tiles_in, grad_out, gate, expert_id, w_conv, w_depth, w_out)


def solution(mesh):
    in_specs = (
        P("expert", None, None, "chan"),
        P("expert", None, None, "chan"),
        P("expert"),
        P("expert", None),
        P("expert", None, None, None, "chan"),
        P("expert", None, "chan"),
        P("expert", "chan", None),
    )
    out_specs = (P("expert", None, None, "chan"), P("expert"))
    return jax.shard_map(
        choose, mesh=mesh, in_specs=in_specs, out_specs=out_specs, check_vma=False
    )
```

```python
import functools
import jax
import jax.numpy as jnp
import numpy as np
from jax import lax
from jax.experimental import pallas as pl
from jax.experimental.pallas import tpu as pltpu
from jax.sharding import PartitionSpec as P

CAP = 2


def group_conv(field, kernel, count):
    return lax.conv_general_dilated(
        field,
        kernel,
        (1, 1),
        "SAME",
        dimension_numbers=("NHWC", "HWIO", "NHWC"),
        feature_group_count=count,
        preferred_element_type=jnp.float32,
    )


def conv_back(field, kernel, count, cotangent):
    forward_value, pullback = jax.vjp(lambda value: group_conv(value, kernel, count), field)
    return pullback(cotangent)[0]


def gelu_slope(value):
    normal_cdf = 0.5 * (1.0 + jax.scipy.special.erf(value * 0.7071067811865476))
    return normal_cdf + value * jnp.exp(-0.5 * value * value) * 0.3989422804014327


def depth_forward(field, taps):
    side = field.shape[1]
    padded = jnp.pad(field, ((0, 0), (1, 1), (1, 1), (0, 0))).astype(jnp.float32)
    total = jnp.zeros(field.shape, jnp.float32)
    for row_off in range(3):
        for col_off in range(3):
            total = total + padded[:, row_off : row_off + side, col_off : col_off + side, :] * taps[
                3 * row_off + col_off
            ].astype(jnp.float32)
    return total


def depth_back(field, taps):
    side = field.shape[1]
    padded = jnp.pad(field, ((0, 0), (1, 1), (1, 1), (0, 0))).astype(jnp.float32)
    total = jnp.zeros(field.shape, jnp.float32)
    for row_off in range(3):
        for col_off in range(3):
            total = total + padded[
                :, 2 - row_off : 2 - row_off + side, 2 - col_off : 2 - col_off + side, :
            ] * taps[3 * row_off + col_off].astype(jnp.float32)
    return total


def on_device_plain(tiles_in, grad_out, gate, expert_id, w_conv, w_depth, w_out):
    owned, side = (tiles_in.shape[0], tiles_in.shape[1])
    local_feat = tiles_in.shape[3]
    sections = lax.axis_size("expert")
    capacity = CAP
    slots = sections * capacity
    chosen = expert_id[:, 0]
    matches = (chosen[:, None] == jnp.arange(sections, dtype=jnp.int32)[None, :]).astype(jnp.int32)
    rows_idx = jnp.arange(owned, dtype=jnp.int32)
    earlier = (rows_idx[:, None] > rows_idx[None, :]).astype(jnp.int32)
    before = jnp.dot(earlier, matches)
    rank = jnp.sum(before * matches, axis=1)
    slot = chosen * capacity + rank
    placing = (slot[:, None] == jnp.arange(slots, dtype=jnp.int32)[None, :]).astype(jnp.bfloat16)
    flat = jnp.concatenate([tiles_in.reshape(owned, -1), grad_out.reshape(owned, -1)], axis=1)
    outward = lax.dot_general(
        placing, flat, (((0,), (0,)), ((), ())), preferred_element_type=jnp.float32
    ).astype(jnp.bfloat16)
    gate_out = lax.dot_general(
        placing,
        gate.reshape(owned, 1),
        (((0,), (0,)), ((), ())),
        preferred_element_type=jnp.float32,
    ).astype(jnp.bfloat16)
    arrived, gate_in = (
        lax.all_to_all(
            outward.reshape(sections, capacity, -1),
            "expert",
            split_axis=0,
            concat_axis=0,
            tiled=True,
        ),
        lax.all_to_all(
            gate_out.reshape(sections, capacity), "expert", split_axis=0, concat_axis=0, tiled=True
        ),
    )
    width = side * side * local_feat
    arrived = arrived.reshape(slots, 2 * width)
    inputs = arrived[:, :width].reshape(slots, side, side, local_feat)
    grads = arrived[:, width:].reshape(slots, side, side, local_feat)
    gates = gate_in.reshape(slots).astype(jnp.float32)
    kernel = w_conv[0]
    taps = w_depth[0]
    project = w_out[0]
    hidden = project.shape[0]
    count = local_feat // kernel.shape[2]
    h_one = group_conv(inputs, kernel, count)
    active = jax.nn.gelu(h_one, approximate=False).astype(jnp.bfloat16)
    h_two = depth_forward(active, taps).astype(jnp.bfloat16)
    gathered = lax.all_gather(grads, "chan", axis=3, tiled=True)
    upper = lax.dot_general(
        gathered.reshape(slots * side * side, -1),
        project,
        (((1,), (1,)), ((), ())),
        preferred_element_type=jnp.float32,
    )
    upper = upper.reshape(slots, side, side, hidden)
    partial_grad = jnp.sum(h_two.astype(jnp.float32) * upper, axis=(1, 2, 3))
    gate_grad = lax.psum(partial_grad, "chan").astype(jnp.bfloat16)
    d_two = (gates[:, None, None, None] * upper).astype(jnp.bfloat16)
    d_act = depth_back(d_two, taps)
    d_one = (d_act * gelu_slope(h_one)).astype(jnp.bfloat16)
    d_input = conv_back(inputs, kernel, count, d_one.astype(jnp.float32))
    back_rows, back_gate = (
        lax.all_to_all(
            d_input.reshape(sections, capacity, -1),
            "expert",
            split_axis=0,
            concat_axis=0,
            tiled=True,
        ),
        lax.all_to_all(
            gate_grad.reshape(sections, capacity), "expert", split_axis=0, concat_axis=0, tiled=True
        ),
    )
    grad_input = jnp.dot(
        placing, back_rows.reshape(slots, -1), preferred_element_type=jnp.float32
    ).astype(jnp.bfloat16)
    grad_gate = jnp.dot(
        placing, back_gate.reshape(slots, 1), preferred_element_type=jnp.float32
    ).astype(jnp.bfloat16)
    return (grad_input.reshape(owned, side, side, local_feat), grad_gate.reshape(owned))


LANES = 128
GROUP_OUT = 256
MESH = pl.DeviceIdType.MESH


def offsets(side):
    found = []
    for row in range(-1, 2):
        for col in range(-1, 2):
            found.append((row, col))
    return found


def shifted(side, position, row, col):
    at_row, at_col = position // side + row, position % side + col
    if 0 <= at_row < side and 0 <= at_col < side:
        return at_row * side + at_col
    return None


def by_quarter(quarter, parts):
    shape = next(part for part in parts if part is not None).shape
    total = None
    for index, part in enumerate(parts):
        part = jnp.zeros(shape, jnp.float32) if part is None else part
        total = part if total is None else jnp.where(quarter == index, part, total)
    return total


def normal_parts(value):
    bell = jnp.exp(-0.5 * value * value)
    turn = 1.0 / (1.0 + 0.23164188 * jnp.abs(value))
    series = 0.5307027145
    for factor in (-0.7265760135, 0.7107068705, -0.142248368, 0.127414796):
        series = series * turn + factor
    tail = series * turn * bell
    return jnp.where(value < 0.0, tail, 1.0 - tail), bell * 0.3989422804014327


def depth_sum(side, field, taps, sign):
    sums = []
    for spot in range(side * side):
        total = None
        for index, (row, col) in enumerate(offsets(side)):
            source = shifted(side, spot, sign * row, sign * col)
            if source is not None:
                term = field[source] * taps[index]
                total = term if total is None else total + term
        sums.append(total)
    return sums


def slot_codes(ids_ref, owned, piece, tiles_t):
    names = [ids_ref[tile] for tile in range(owned)]
    codes = []
    for tile in range(owned):
        rank = jnp.int32(0)
        for earlier in range(tile):
            rank = rank + jnp.where(names[earlier] == names[tile], 1, 0)
        codes.append(names[tile] * piece + rank * tiles_t)
    return codes


def target(base, codes):
    total = base & 0xFFFF
    at_tile = base >> 16
    for tile, code in enumerate(codes):
        total = total + jnp.where(at_tile == tile, code, 0)
    return total


def owner_kernel(dims, ids_ref, base_col_ref, back_ref, out_ref, gate_out_ref):
    n_e, n_c, owned, tiles_t, side = dims
    spots = side * side
    pairs = (spots + 1) // 2
    piece = 2 * CAP * tiles_t
    strip = 2 * owned
    rows_here, rows_routed = 2 * owned * tiles_t, n_e * piece
    codes = slot_codes(ids_ref, owned, piece, tiles_t)
    place_back = jnp.where(
        lax.broadcasted_iota(jnp.int32, (rows_here, rows_routed), 1)
        == target(base_col_ref[...], codes),
        1.0,
        0.0,
    ).astype(jnp.bfloat16)
    for pair in range(pairs):
        got = back_ref[:, pair].reshape(rows_routed, LANES)
        got = jnp.dot(place_back, got, preferred_element_type=jnp.float32)
        got = jnp.concatenate([got[at * strip : (at + 1) * strip] for at in range(tiles_t)], axis=1)
        if pair < pairs - 1:
            out_ref[pair * strip : (pair + 1) * strip] = got.astype(jnp.bfloat16)
        else:
            out_ref[pair * strip :] = got[:owned].astype(jnp.bfloat16)
            rows = got[owned:, :owned]
    diagonal = lax.broadcasted_iota(jnp.int32, (owned, owned), 0) == lax.broadcasted_iota(
        jnp.int32, (owned, owned), 1
    )
    gate_row = jnp.sum(jnp.where(diagonal, rows, 0.0), axis=0, keepdims=True)
    gate_out_ref[...] = gate_row.astype(jnp.bfloat16).reshape(gate_out_ref.shape)


def expert_kernel(
    dims,
    ids_ref,
    x_ref,
    g_ref,
    gate_ref,
    base_row_ref,
    order_ref,
    order_back_ref,
    taps_ref,
    wc_hbm,
    wo_hbm,
    back_ref,
    wc,
    wo,
    flat,
    zbuf,
    send,
    recv,
    xbuf,
    gbuf,
    xcol,
    h2,
    slope,
    partial_first,
    partial_second,
    upper_even,
    upper_odd,
    dz,
    gates,
    wc_sem,
    wo_sem,
    zsend_sem,
    zrecv_sem,
    send_sem,
    recv_sem,
    gsend_sem,
    grecv_sem,
    own_sem,
):
    n_e, n_c, owned, tiles_t, side = dims
    spots = side * side
    pairs = (spots + 1) // 2
    slots = n_e * CAP
    groups = wc.shape[1] // GROUP_OUT
    per_t = groups // tiles_t
    width = tiles_t * LANES
    piece = 2 * CAP * tiles_t
    me, z = lax.axis_index("expert"), lax.axis_index("chan")
    partial = (partial_first, partial_second)
    offs = offsets(side)
    taps_used = len(offs)

    order = []
    for step in range(n_c):
        block = 0
        for at in range(n_c):
            ranked = sorted(range(n_c), key=lambda other: (abs(other - at), other if 2 * at < n_c else -other))
            block = block + jnp.where(z == at, ranked[step], 0)
        order.append(block)

    wc_copy = pltpu.make_async_copy(wc_hbm, wc.at[pl.ds(0, wc_hbm.shape[0])], wc_sem)
    wc_copy.start()
    wo_copies = []
    for step in range(n_c):
        start = pl.multiple_of(order[step] * width, width)
        wo_copies.append(
            pltpu.make_async_copy(wo_hbm.at[:, pl.ds(start, width)], wo.at[step], wo_sem.at[step])
        )
        wo_copies[step].start()

    barrier = pltpu.get_barrier_semaphore()
    for step in range(1, n_e):
        pl.semaphore_signal(
            barrier, inc=1, device_id=(lax.rem(me + step, n_e), z), device_id_type=MESH
        )
    for step in range(1, n_c):
        pl.semaphore_signal(
            barrier, inc=1, device_id=(me, lax.rem(z + step, n_c)), device_id_type=MESH
        )

    wc[pl.ds(wc_hbm.shape[0], wc.shape[0] - wc_hbm.shape[0])] = jnp.zeros(
        (wc.shape[0] - wc_hbm.shape[0], wc.shape[1]), jnp.bfloat16
    )

    codes = slot_codes(ids_ref, owned, piece, tiles_t)
    rows_here, rows_routed = 2 * owned * tiles_t, n_e * piece

    place = jnp.where(
        lax.broadcasted_iota(jnp.int32, (rows_routed, rows_here), 0) == target(base_row_ref[...], codes),
        1.0,
        0.0,
    ).astype(jnp.bfloat16)

    strip = 2 * owned

    def route(block, field):
        for pair in range(pairs):
            taken = field[pair * strip : (pair + 1) * strip, :]
            taken = jnp.concatenate(
                [taken[:, at * LANES : (at + 1) * LANES] for at in range(tiles_t)], axis=0
            )
            routed = jnp.dot(place, taken, preferred_element_type=jnp.float32)
            send[block, :, pair] = routed.astype(jnp.bfloat16).reshape(n_e, piece, LANES)

    def exchange(block):
        copies = []
        for step in range(1, n_e):
            peer = lax.rem(me + step, n_e)
            copies.append(
                pltpu.make_async_remote_copy(
                    src_ref=send.at[block, peer],
                    dst_ref=back_ref.at[me] if block == back_block else recv.at[block, me],
                    send_sem=send_sem.at[block, step],
                    recv_sem=recv_sem.at[block, step],
                    device_id=(peer, z),
                    device_id_type=MESH,
                )
            )
        return copies

    def keep_own(block):
        recv[block, me] = send[block, me]

    def unroute(block, store):
        for pair in range(pairs):
            got = recv[block, :, pair].reshape(rows_routed, LANES)
            got = jnp.dot(order_ref[...], got, preferred_element_type=jnp.float32)
            store(pair, got.astype(jnp.bfloat16).reshape(2, tiles_t, slots, LANES))

    def z_copy(block, toward):
        return pltpu.make_async_remote_copy(
            src_ref=zbuf.at[block],
            dst_ref=zbuf.at[block],
            send_sem=zsend_sem.at[block, (toward + 1) // 2],
            recv_sem=zrecv_sem.at[block],
            device_id=(me, z + toward),
            device_id_type=MESH,
        )

    x_block = n_c
    back_block = n_c + 1
    zbuf[z] = jnp.concatenate(
        [g_ref[...].astype(jnp.float32), jnp.zeros((owned, width), jnp.float32)], axis=0
    ).astype(jnp.bfloat16)
    diagonal = lax.broadcasted_iota(jnp.int32, (owned, owned), 0) == lax.broadcasted_iota(
        jnp.int32, (owned, owned), 1
    )
    spread_gate = jnp.where(diagonal, gate_ref[...].astype(jnp.float32), 0.0)
    spread_gate = jnp.broadcast_to(jnp.sum(spread_gate, axis=1, keepdims=True), (owned, width))
    flat[...] = jnp.concatenate(
        [x_ref[...].astype(jnp.float32), spread_gate], axis=0
    ).astype(jnp.bfloat16)
    route(x_block, flat)
    keep_own(x_block)
    pl.semaphore_wait(barrier, n_e - 1 + n_c - 1)

    @pl.when(z > 0)
    def _():
        z_copy(z, -1).start()

    @pl.when(z < n_c - 1)
    def _():
        z_copy(z, 1).start()

    all_copies = {}
    all_copies[x_block] = exchange(x_block)
    for copy in all_copies[x_block]:
        copy.start()
    route(0, zbuf.at[z])
    keep_own(0)
    all_copies[0] = exchange(0)
    for copy in all_copies[0]:
        copy.start()

    def take_z(step):
        block = order[step]
        z_copy(block, 1).wait_recv()

        @pl.when((block < z) & (z < n_c - 1))
        def _():
            z_copy(block, 1).start()

        @pl.when((block > z) & (z > 0))
        def _():
            z_copy(block, -1).start()

        route(step, zbuf.at[block])
        keep_own(step)
        all_copies[step] = exchange(step)
        for copy in all_copies[step]:
            copy.start()

    def taps_at(group, cut):
        start = pl.multiple_of(group * GROUP_OUT + cut * LANES, LANES)
        taps = taps_ref[:, pl.ds(start, LANES)].astype(jnp.float32)
        return [
            jnp.broadcast_to(taps[index : index + 1], (slots, LANES)).astype(jnp.bfloat16)
            for index in range(taps_used)
        ]

    def project(step, group):
        rows = pl.ds(pl.multiple_of(group * GROUP_OUT, GROUP_OUT), GROUP_OUT)
        return lax.dot_general(
            gbuf[step], wo[step, rows], (((1,), (1,)), ((), ())), preferred_element_type=jnp.float32
        )

    def take_block(step):
        for copy in all_copies[step]:
            copy.wait_recv()

        def store(pair, value):
            for parity in range(2):
                spot = 2 * pair + parity
                if spot < spots:
                    for tile_t in range(tiles_t):
                        gbuf[
                            step,
                            spot * slots : (spot + 1) * slots,
                            tile_t * LANES : (tile_t + 1) * LANES,
                        ] = value[parity, tile_t]

        unroute(step, store)
        wo_copies[step].wait()

    quarter = lax.broadcasted_iota(jnp.int32, (slots, LANES), 1) // (LANES // per_t)
    half = LANES // per_t

    def forward(tile_t, first, step):
        field = jnp.concatenate([xbuf[tile_t, spot] for spot in range(spots)], axis=0).astype(jnp.float32)
        turned = [field] + [pltpu.roll(field, half * turn, 1) for turn in range(1, per_t)]

        def part(turn, spot):
            return None if spot is None else turned[turn][spot * slots : (spot + 1) * slots]

        for inner in range(per_t):
            for spot in range(spots):
                for lane_tile in range(wc.shape[0] // LANES):
                    parts = []
                    for at in range(per_t):
                        offset = lane_tile * per_t + at
                        source = shifted(side, spot, *offs[offset]) if offset < taps_used else None
                        parts.append(part((at - inner) % per_t, source))
                    if all(item is None for item in parts):
                        value = jnp.zeros((slots, LANES), jnp.float32)
                    else:
                        value = by_quarter(quarter, parts)
                    xcol[
                        inner,
                        spot * slots : (spot + 1) * slots,
                        lane_tile * LANES : (lane_tile + 1) * LANES,
                    ] = value.astype(jnp.bfloat16)

        def each(inner, carry):
            group = tile_t * per_t + inner
            lanes = pl.ds(pl.multiple_of(group * GROUP_OUT, GROUP_OUT), GROUP_OUT)
            h_one = jnp.dot(xcol[inner], wc[:, lanes], preferred_element_type=jnp.float32)
            if step is not None:
                for part in range(2):
                    ahead = 2 * ((tile_t - first) * per_t + inner) + part
                    partial[step][ahead] = project(step, ahead)
            for cut in range(GROUP_OUT // LANES):
                value = h_one[:, cut * LANES : (cut + 1) * LANES]
                cdf, density = normal_parts(value)
                slant = cdf + value * density
                slope[group, :, cut * LANES : (cut + 1) * LANES] = slant
                active = (value * cdf).astype(jnp.bfloat16)
                active = [active[spot * slots : (spot + 1) * slots] for spot in range(spots)]
                for spot, total in enumerate(depth_sum(side, active, taps_at(group, cut), 1)):
                    h2[
                        group, spot * slots : (spot + 1) * slots, cut * LANES : (cut + 1) * LANES
                    ] = total
            return carry

        for inner in range(per_t):
            each(inner, 0)

    if n_c > 1:
        take_z(1)
    for copy in all_copies[x_block]:
        copy.wait_recv()

    def store_x(pair, value):
        for parity in range(2):
            for tile_t in range(tiles_t):
                xbuf[tile_t, 2 * pair + parity] = value[parity, tile_t]

    unroute(x_block, store_x)
    wc_copy.wait()
    early = min(2, n_c - 1)
    middle = tiles_t // 2
    for half_at in range(2):
        step = half_at if half_at < early else None
        first, last = (middle, tiles_t) if half_at else (0, middle)
        if step is not None:
            take_block(step)

        def walk(tile_t, carry):
            forward(tile_t, first, step)
            return carry

        if half_at:
            lax.fori_loop(first, last, walk, 0)
        else:
            for tile_t in range(first, last):
                walk(tile_t, 0)
                for at in range(2, n_c):
                    if at - 2 == tile_t or (tile_t == last - 1 and at - 2 > tile_t):
                        take_z(at)
    for step in range(early, n_c):
        take_block(step)

    gate = xbuf[0, spots].astype(jnp.float32)
    uppers = (upper_even, upper_odd)

    def finish(tile_t, carry):
        for inner in range(per_t):
            group = tile_t * per_t + inner
            product = None
            for step in range(early, n_c):
                term = project(step, group)
                product = term if product is None else product + term
            for step in range(early):
                product = product + partial[step][group]
            uppers[tile_t % 2][inner] = product
            both = product * h2[group].astype(jnp.float32)
            for spot in range(spots):
                for cut in range(GROUP_OUT // LANES):
                    carry = carry + both[
                        spot * slots : (spot + 1) * slots, cut * LANES : (cut + 1) * LANES
                    ]
        return carry

    def backward(tile_t):
        folded = []
        for inner in range(per_t):
            group = tile_t * per_t + inner
            lanes = pl.ds(pl.multiple_of(group * GROUP_OUT, GROUP_OUT), GROUP_OUT)
            sides = []
            for cut in range(GROUP_OUT // LANES):
                where = slice(cut * LANES, (cut + 1) * LANES)
                d_two = [
                    (gate * uppers[tile_t % 2][inner, spot * slots : (spot + 1) * slots, where]).astype(
                        jnp.bfloat16
                    )
                    for spot in range(spots)
                ]
                done = []
                for spot, total in enumerate(depth_sum(side, d_two, taps_at(group, cut), -1)):
                    slant = slope[group, spot * slots : (spot + 1) * slots, where]
                    done.append((total.astype(jnp.float32) * slant).astype(jnp.bfloat16))
                sides.append(jnp.concatenate(done, axis=0))
            d_one = jnp.concatenate(sides, axis=1)
            spread = lax.dot_general(
                d_one, wc[:, lanes], (((1,), (1,)), ((), ())), preferred_element_type=jnp.float32
            )
            sums = []
            for spot in range(spots):
                total = None
                for lane_tile in range(wc.shape[0] // LANES):
                    parts = []
                    for at in range(per_t):
                        offset = lane_tile * per_t + at
                        source = None
                        if offset < taps_used:
                            source = shifted(side, spot, -offs[offset][0], -offs[offset][1])
                        parts.append(
                            None
                            if source is None
                            else spread[
                                source * slots : (source + 1) * slots,
                                lane_tile * LANES : (lane_tile + 1) * LANES,
                            ]
                        )
                    if any(item is not None for item in parts):
                        value = by_quarter(quarter, parts)
                        total = value if total is None else total + value
                sums.append(total)
            folded.append(sums)
        for spot in range(spots):
            total = None
            for turn in range(per_t):
                value = by_quarter(
                    quarter, [folded[(at + turn) % per_t][spot] for at in range(per_t)]
                )
                value = pltpu.roll(value, half * turn, 1) if turn else value
                total = value if total is None else total + value
            dz[spot, tile_t] = total.astype(jnp.bfloat16)

    summed = finish(0, jnp.zeros((slots, LANES), jnp.float32))
    for tile_t in range(tiles_t - 1):
        summed = finish(tile_t + 1, summed)
        backward(tile_t)
    gates[z] = summed
    gate_copies = []
    for step in range(1, n_c):
        gate_copies.append(
            pltpu.make_async_remote_copy(
                src_ref=gates.at[z],
                dst_ref=gates.at[z],
                send_sem=gsend_sem.at[step],
                recv_sem=grecv_sem.at[step],
                device_id=(me, lax.rem(z + step, n_c)),
                device_id_type=MESH,
            )
        )
        gate_copies[-1].start()

    backward(tiles_t - 1)
    for copy in gate_copies:
        copy.wait_recv()
    total = gates[0]
    for at in range(1, n_c):
        total = total + gates[at]
    total = jnp.broadcast_to(jnp.sum(total, axis=1, keepdims=True), (slots, LANES))
    for tile_t in range(tiles_t):
        dz[spots, tile_t] = total.astype(jnp.bfloat16)

    for pair in range(pairs):
        field = dz[2 * pair : 2 * pair + 2].reshape(rows_routed, LANES)
        field = jnp.dot(order_back_ref[...], field, preferred_element_type=jnp.float32)
        send[back_block, :, pair] = field.astype(jnp.bfloat16).reshape(n_e, piece, LANES)
    all_copies[back_block] = exchange(back_block)
    for copy in all_copies[back_block]:
        copy.start()
    own_copy = pltpu.make_async_copy(send.at[back_block, me], back_ref.at[me], own_sem)
    own_copy.start()
    for copy in all_copies[back_block]:
        copy.wait_recv()
    own_copy.wait()

    for block in all_copies:
        for copy in all_copies[block]:
            copy.wait_send()
    for copy in gate_copies:
        copy.wait_send()

    @pl.when(z > 0)
    def _():
        z_copy(z, -1).wait_send()

    @pl.when(z < n_c - 1)
    def _():
        z_copy(z, 1).wait_send()

    for step in range(1, n_c):
        block = order[step]

        @pl.when((block < z) & (z < n_c - 1))
        def _():
            z_copy(block, 1).wait_send()

        @pl.when((block > z) & (z > 0))
        def _():
            z_copy(block, -1).wait_send()


def on_device(tiles_in, grad_out, gate, expert_id, w_conv, w_depth, w_out):
    owned, side, local_feat = tiles_in.shape[0], tiles_in.shape[1], tiles_in.shape[3]
    n_e, n_c = lax.axis_size("expert"), lax.axis_size("chan")
    hidden = w_out.shape[1]
    tiles_t = local_feat // LANES
    spots = side * side
    pairs = (spots + 1) // 2
    slots = n_e * CAP
    piece = 2 * CAP * tiles_t
    groups = hidden // GROUP_OUT
    group_in = w_conv.shape[3]
    rows_here, rows_routed = 2 * owned * tiles_t, n_e * piece

    column = np.arange(rows_here)
    lane_t, parity, tile = column // (2 * owned), column // owned % 2, column % owned
    base = (tile << 16) + parity * CAP * tiles_t + lane_t
    base_row = jnp.asarray(base.reshape(1, -1), jnp.int32)
    base_col = jnp.asarray(base.reshape(-1, 1), jnp.int32)
    row = np.arange(rows_routed)
    parity, lane_t = row // (tiles_t * slots), row // slots % tiles_t
    source, rank = row % slots // CAP, row % CAP
    order = np.zeros((rows_routed, rows_routed), np.float32)
    order[row, ((source * 2 + parity) * CAP + rank) * tiles_t + lane_t] = 1.0
    taps_rows = 9 * group_in
    padded_rows = -(-taps_rows // LANES) * LANES
    dims = (n_e, n_c, owned, tiles_t, side)
    vmem = pl.BlockSpec(memory_space=pltpu.VMEM)
    anywhere = pl.BlockSpec(memory_space=pl.ANY)
    blocks = n_c + 2
    bf16, f32 = jnp.bfloat16, jnp.float32
    ids = expert_id.reshape(owned)
    back = pl.pallas_call(
        functools.partial(expert_kernel, dims),
        out_shape=jax.ShapeDtypeStruct((n_e, pairs, piece, LANES), bf16),
        in_specs=[pl.BlockSpec(memory_space=pltpu.SMEM)] + [vmem] * 7 + [anywhere] * 2,
        out_specs=anywhere,
        scratch_shapes=[
            pltpu.VMEM((padded_rows, hidden), bf16),
            pltpu.VMEM((n_c, hidden, local_feat), bf16),
            pltpu.VMEM((2 * pairs * owned, local_feat), bf16),
            pltpu.VMEM((n_c, 2 * pairs * owned, local_feat), bf16),
            pltpu.VMEM((blocks, n_e, pairs, piece, LANES), bf16),
            pltpu.VMEM((blocks - 1, n_e, pairs, piece, LANES), bf16),
            pltpu.VMEM((tiles_t, 2 * pairs, slots, LANES), bf16),
            pltpu.VMEM((n_c, spots * slots, local_feat), bf16),
            pltpu.VMEM((LANES // group_in, spots * slots, padded_rows), bf16),
            pltpu.VMEM((groups, spots * slots, GROUP_OUT), bf16),
            pltpu.VMEM((groups, spots * slots, GROUP_OUT), f32),
            pltpu.VMEM((groups, spots * slots, GROUP_OUT), f32),
            pltpu.VMEM((groups, spots * slots, GROUP_OUT), f32),
            pltpu.VMEM((groups // tiles_t, spots * slots, GROUP_OUT), f32),
            pltpu.VMEM((groups // tiles_t, spots * slots, GROUP_OUT), f32),
            pltpu.VMEM((2 * pairs, tiles_t, slots, LANES), bf16),
            pltpu.VMEM((n_c, slots, LANES), f32),
            pltpu.SemaphoreType.DMA,
            pltpu.SemaphoreType.DMA((n_c,)),
            pltpu.SemaphoreType.DMA((n_c, 2)),
            pltpu.SemaphoreType.DMA((n_c,)),
            pltpu.SemaphoreType.DMA((blocks, n_e)),
            pltpu.SemaphoreType.DMA((blocks, n_e)),
            pltpu.SemaphoreType.DMA((n_c,)),
            pltpu.SemaphoreType.DMA((n_c,)),
            pltpu.SemaphoreType.DMA,
        ],
        compiler_params=pltpu.CompilerParams(
            collective_id=0, has_side_effects=True, vmem_limit_bytes=56 * 1024 * 1024
        ),
    )(
        ids,
        tiles_in.transpose(1, 2, 0, 3).reshape(spots * owned, local_feat),
        grad_out.transpose(1, 2, 0, 3).reshape(spots * owned, local_feat),
        gate.reshape(1, owned),
        base_row,
        jnp.asarray(order, bf16),
        jnp.asarray(order.T, bf16),
        w_depth.reshape(9, hidden),
        w_conv.reshape(taps_rows, hidden),
        w_out.reshape(hidden, w_out.shape[2]),
    )
    grad_input, grad_gate = pl.pallas_call(
        functools.partial(owner_kernel, dims),
        out_shape=(
            jax.ShapeDtypeStruct((spots * owned, local_feat), bf16),
            jax.ShapeDtypeStruct((owned,), bf16),
        ),
        in_specs=[pl.BlockSpec(memory_space=pltpu.SMEM), vmem, vmem],
        out_specs=(vmem, vmem),
    )(ids, base_col, back)
    grad_input = grad_input.reshape(side, side, owned, local_feat).transpose(2, 0, 1, 3)
    return grad_input, grad_gate


def choose(tiles_in, grad_out, gate, expert_id, w_conv, w_depth, w_out):
    owned, side, local_feat = tiles_in.shape[0], tiles_in.shape[1], tiles_in.shape[3]
    count = local_feat // w_conv.shape[3]
    whole = local_feat % LANES == 0 and 2 * CAP * (local_feat // LANES) % 16 == 0
    whole = whole and lax.axis_size("expert") * CAP % 16 == 0 and side % 2 == 1 and owned % 8 == 0
    whole = whole and w_out.shape[1] == count * GROUP_OUT and LANES % w_conv.shape[3] == 0
    body = on_device if whole else on_device_plain
    return body(tiles_in, grad_out, gate, expert_id, w_conv, w_depth, w_out)


def solution(mesh):
    in_specs = (
        P("expert", None, None, "chan"),
        P("expert", None, None, "chan"),
        P("expert"),
        P("expert", None),
        P("expert", None, None, None, "chan"),
        P("expert", None, "chan"),
        P("expert", "chan", None),
    )
    out_specs = (P("expert", None, None, "chan"), P("expert"))
    return jax.shard_map(
        choose, mesh=mesh, in_specs=in_specs, out_specs=out_specs, check_vma=False
    )
```

```python
import functools
import jax
import jax.numpy as jnp
import numpy as np
from jax import lax
from jax.experimental import pallas as pl
from jax.experimental.pallas import tpu as pltpu
from jax.sharding import PartitionSpec as P

CAP = 2


def group_conv(field, kernel, count):
    return lax.conv_general_dilated(
        field,
        kernel,
        (1, 1),
        "SAME",
        dimension_numbers=("NHWC", "HWIO", "NHWC"),
        feature_group_count=count,
        preferred_element_type=jnp.float32,
    )


def conv_back(field, kernel, count, cotangent):
    forward_value, pullback = jax.vjp(lambda value: group_conv(value, kernel, count), field)
    return pullback(cotangent)[0]


def gelu_slope(value):
    normal_cdf = 0.5 * (1.0 + jax.scipy.special.erf(value * 0.7071067811865476))
    return normal_cdf + value * jnp.exp(-0.5 * value * value) * 0.3989422804014327


def depth_forward(field, taps):
    side = field.shape[1]
    padded = jnp.pad(field, ((0, 0), (1, 1), (1, 1), (0, 0))).astype(jnp.float32)
    total = jnp.zeros(field.shape, jnp.float32)
    for row_off in range(3):
        for col_off in range(3):
            total = total + padded[:, row_off : row_off + side, col_off : col_off + side, :] * taps[
                3 * row_off + col_off
            ].astype(jnp.float32)
    return total


def depth_back(field, taps):
    side = field.shape[1]
    padded = jnp.pad(field, ((0, 0), (1, 1), (1, 1), (0, 0))).astype(jnp.float32)
    total = jnp.zeros(field.shape, jnp.float32)
    for row_off in range(3):
        for col_off in range(3):
            total = total + padded[
                :, 2 - row_off : 2 - row_off + side, 2 - col_off : 2 - col_off + side, :
            ] * taps[3 * row_off + col_off].astype(jnp.float32)
    return total


def on_device_plain(tiles_in, grad_out, gate, expert_id, w_conv, w_depth, w_out):
    owned, side = (tiles_in.shape[0], tiles_in.shape[1])
    local_feat = tiles_in.shape[3]
    sections = lax.axis_size("expert")
    capacity = CAP
    slots = sections * capacity
    chosen = expert_id[:, 0]
    matches = (chosen[:, None] == jnp.arange(sections, dtype=jnp.int32)[None, :]).astype(jnp.int32)
    rows_idx = jnp.arange(owned, dtype=jnp.int32)
    earlier = (rows_idx[:, None] > rows_idx[None, :]).astype(jnp.int32)
    before = jnp.dot(earlier, matches)
    rank = jnp.sum(before * matches, axis=1)
    slot = chosen * capacity + rank
    placing = (slot[:, None] == jnp.arange(slots, dtype=jnp.int32)[None, :]).astype(jnp.bfloat16)
    flat = jnp.concatenate([tiles_in.reshape(owned, -1), grad_out.reshape(owned, -1)], axis=1)
    outward = lax.dot_general(
        placing, flat, (((0,), (0,)), ((), ())), preferred_element_type=jnp.float32
    ).astype(jnp.bfloat16)
    gate_out = lax.dot_general(
        placing,
        gate.reshape(owned, 1),
        (((0,), (0,)), ((), ())),
        preferred_element_type=jnp.float32,
    ).astype(jnp.bfloat16)
    arrived, gate_in = (
        lax.all_to_all(
            outward.reshape(sections, capacity, -1),
            "expert",
            split_axis=0,
            concat_axis=0,
            tiled=True,
        ),
        lax.all_to_all(
            gate_out.reshape(sections, capacity), "expert", split_axis=0, concat_axis=0, tiled=True
        ),
    )
    width = side * side * local_feat
    arrived = arrived.reshape(slots, 2 * width)
    inputs = arrived[:, :width].reshape(slots, side, side, local_feat)
    grads = arrived[:, width:].reshape(slots, side, side, local_feat)
    gates = gate_in.reshape(slots).astype(jnp.float32)
    kernel = w_conv[0]
    taps = w_depth[0]
    project = w_out[0]
    hidden = project.shape[0]
    count = local_feat // kernel.shape[2]
    h_one = group_conv(inputs, kernel, count)
    active = jax.nn.gelu(h_one, approximate=False).astype(jnp.bfloat16)
    h_two = depth_forward(active, taps).astype(jnp.bfloat16)
    gathered = lax.all_gather(grads, "chan", axis=3, tiled=True)
    upper = lax.dot_general(
        gathered.reshape(slots * side * side, -1),
        project,
        (((1,), (1,)), ((), ())),
        preferred_element_type=jnp.float32,
    )
    upper = upper.reshape(slots, side, side, hidden)
    partial_grad = jnp.sum(h_two.astype(jnp.float32) * upper, axis=(1, 2, 3))
    gate_grad = lax.psum(partial_grad, "chan").astype(jnp.bfloat16)
    d_two = (gates[:, None, None, None] * upper).astype(jnp.bfloat16)
    d_act = depth_back(d_two, taps)
    d_one = (d_act * gelu_slope(h_one)).astype(jnp.bfloat16)
    d_input = conv_back(inputs, kernel, count, d_one.astype(jnp.float32))
    back_rows, back_gate = (
        lax.all_to_all(
            d_input.reshape(sections, capacity, -1),
            "expert",
            split_axis=0,
            concat_axis=0,
            tiled=True,
        ),
        lax.all_to_all(
            gate_grad.reshape(sections, capacity), "expert", split_axis=0, concat_axis=0, tiled=True
        ),
    )
    grad_input = jnp.dot(
        placing, back_rows.reshape(slots, -1), preferred_element_type=jnp.float32
    ).astype(jnp.bfloat16)
    grad_gate = jnp.dot(
        placing, back_gate.reshape(slots, 1), preferred_element_type=jnp.float32
    ).astype(jnp.bfloat16)
    return (grad_input.reshape(owned, side, side, local_feat), grad_gate.reshape(owned))


LANES = 128
GROUP_OUT = 256
MESH = pl.DeviceIdType.MESH


def offsets(side):
    found = []
    for row in range(-1, 2):
        for col in range(-1, 2):
            found.append((row, col))
    return found


def shifted(side, position, row, col):
    at_row, at_col = position // side + row, position % side + col
    if 0 <= at_row < side and 0 <= at_col < side:
        return at_row * side + at_col
    return None


def by_quarter(quarter, parts):
    shape = next(part for part in parts if part is not None).shape
    total = None
    for index, part in enumerate(parts):
        part = jnp.zeros(shape, jnp.float32) if part is None else part
        total = part if total is None else jnp.where(quarter == index, part, total)
    return total


def slot_codes(ids_ref, owned, piece, tiles_t):
    names = [ids_ref[tile] for tile in range(owned)]
    codes = []
    for tile in range(owned):
        rank = jnp.int32(0)
        for earlier in range(tile):
            rank = rank + jnp.where(names[earlier] == names[tile], 1, 0)
        codes.append(names[tile] * piece + rank * tiles_t)
    return codes


def target(base, codes):
    total = base & 0xFFFF
    at_tile = base >> 16
    for tile, code in enumerate(codes):
        total = total + jnp.where(at_tile == tile, code, 0)
    return total


def owner_kernel(dims, ids_ref, base_col_ref, back_ref, out_ref, gate_out_ref):
    n_e, n_c, owned, tiles_t, side = dims
    spots = side * side
    pairs = (spots + 1) // 2
    piece = 2 * CAP * tiles_t
    strip = 2 * owned
    rows_here, rows_routed = 2 * owned * tiles_t, n_e * piece
    codes = slot_codes(ids_ref, owned, piece, tiles_t)
    place_back = jnp.where(
        lax.broadcasted_iota(jnp.int32, (rows_here, rows_routed), 1)
        == target(base_col_ref[...], codes),
        1.0,
        0.0,
    ).astype(jnp.bfloat16)
    for pair in range(pairs):
        got = back_ref[:, pair].reshape(rows_routed, LANES)
        got = jnp.dot(place_back, got, preferred_element_type=jnp.float32)
        got = jnp.concatenate([got[at * strip : (at + 1) * strip] for at in range(tiles_t)], axis=1)
        if pair < pairs - 1:
            out_ref[pair * strip : (pair + 1) * strip] = got.astype(jnp.bfloat16)
        else:
            out_ref[pair * strip :] = got[:owned].astype(jnp.bfloat16)
            rows = got[owned:, :owned]
    diagonal = lax.broadcasted_iota(jnp.int32, (owned, owned), 0) == lax.broadcasted_iota(
        jnp.int32, (owned, owned), 1
    )
    gate_row = jnp.sum(jnp.where(diagonal, rows, 0.0), axis=0, keepdims=True)
    gate_out_ref[...] = gate_row.astype(jnp.bfloat16).reshape(gate_out_ref.shape)


def expert_kernel(
    dims,
    ids_ref,
    x_ref,
    g_ref,
    gate_ref,
    base_row_ref,
    order_ref,
    order_back_ref,
    taps_ref,
    wc_hbm,
    wo_hbm,
    back_ref,
    wc,
    wo,
    flat,
    zbuf,
    send,
    recv,
    xbuf,
    gbuf,
    xcol,
    h2,
    slope,
    partial_first,
    partial_second,
    partial_third,
    upper_even,
    upper_odd,
    dz,
    gates,
    wc_sem,
    wo_sem,
    zsend_sem,
    zrecv_sem,
    send_sem,
    recv_sem,
    gsend_sem,
    grecv_sem,
    own_sem,
):
    n_e, n_c, owned, tiles_t, side = dims
    spots = side * side
    pairs = (spots + 1) // 2
    slots = n_e * CAP
    groups = wc.shape[1] // GROUP_OUT
    per_t = groups // tiles_t
    width = tiles_t * LANES
    piece = 2 * CAP * tiles_t
    me, z = lax.axis_index("expert"), lax.axis_index("chan")
    partial = (partial_first, partial_second, partial_third)
    offs = offsets(side)
    taps_used = len(offs)

    order = []
    for step in range(n_c):
        block = 0
        for at in range(n_c):
            ranked = sorted(range(n_c), key=lambda other: (abs(other - at), other if 2 * at < n_c else -other))
            block = block + jnp.where(z == at, ranked[step], 0)
        order.append(block)

    wc_copy = pltpu.make_async_copy(wc_hbm, wc.at[pl.ds(0, wc_hbm.shape[0])], wc_sem)
    wc_copy.start()
    wo_copies = []
    for step in range(n_c):
        start = pl.multiple_of(order[step] * width, width)
        wo_copies.append(
            pltpu.make_async_copy(wo_hbm.at[:, pl.ds(start, width)], wo.at[step], wo_sem.at[step])
        )
        wo_copies[step].start()

    barrier = pltpu.get_barrier_semaphore()
    for step in range(1, n_e):
        pl.semaphore_signal(
            barrier, inc=1, device_id=(lax.rem(me + step, n_e), z), device_id_type=MESH
        )
    for step in range(1, n_c):
        pl.semaphore_signal(
            barrier, inc=1, device_id=(me, lax.rem(z + step, n_c)), device_id_type=MESH
        )

    wc[pl.ds(wc_hbm.shape[0], wc.shape[0] - wc_hbm.shape[0])] = jnp.zeros(
        (wc.shape[0] - wc_hbm.shape[0], wc.shape[1]), jnp.bfloat16
    )

    codes = slot_codes(ids_ref, owned, piece, tiles_t)
    rows_here, rows_routed = 2 * owned * tiles_t, n_e * piece

    place = jnp.where(
        lax.broadcasted_iota(jnp.int32, (rows_routed, rows_here), 0) == target(base_row_ref[...], codes),
        1.0,
        0.0,
    ).astype(jnp.bfloat16)

    strip = 2 * owned

    def route(block, field):
        for pair in range(pairs):
            taken = field[pair * strip : (pair + 1) * strip, :]
            taken = jnp.concatenate(
                [taken[:, at * LANES : (at + 1) * LANES] for at in range(tiles_t)], axis=0
            )
            routed = jnp.dot(place, taken, preferred_element_type=jnp.float32)
            send[block, :, pair] = routed.astype(jnp.bfloat16).reshape(n_e, piece, LANES)

    def exchange(block):
        copies = []
        for step in range(1, n_e):
            peer = lax.rem(me + step, n_e)
            copies.append(
                pltpu.make_async_remote_copy(
                    src_ref=send.at[block, peer],
                    dst_ref=back_ref.at[me] if block == back_block else recv.at[block, me],
                    send_sem=send_sem.at[block, step],
                    recv_sem=recv_sem.at[block, step],
                    device_id=(peer, z),
                    device_id_type=MESH,
                )
            )
        return copies

    def keep_own(block):
        recv[block, me] = send[block, me]

    def unroute(block, store):
        for pair in range(pairs):
            got = recv[block, :, pair].reshape(rows_routed, LANES)
            got = jnp.dot(order_ref[...], got, preferred_element_type=jnp.float32)
            store(pair, got.astype(jnp.bfloat16).reshape(2, tiles_t, slots, LANES))

    def z_copy(block, toward):
        return pltpu.make_async_remote_copy(
            src_ref=zbuf.at[block],
            dst_ref=zbuf.at[block],
            send_sem=zsend_sem.at[block, (toward + 1) // 2],
            recv_sem=zrecv_sem.at[block],
            device_id=(me, z + toward),
            device_id_type=MESH,
        )

    x_block = n_c
    back_block = n_c + 1
    zbuf[z] = jnp.concatenate(
        [g_ref[...].astype(jnp.float32), jnp.zeros((owned, width), jnp.float32)], axis=0
    ).astype(jnp.bfloat16)
    diagonal = lax.broadcasted_iota(jnp.int32, (owned, owned), 0) == lax.broadcasted_iota(
        jnp.int32, (owned, owned), 1
    )
    spread_gate = jnp.where(diagonal, gate_ref[...].astype(jnp.float32), 0.0)
    spread_gate = jnp.broadcast_to(jnp.sum(spread_gate, axis=1, keepdims=True), (owned, width))
    flat[...] = jnp.concatenate(
        [x_ref[...].astype(jnp.float32), spread_gate], axis=0
    ).astype(jnp.bfloat16)
    route(x_block, flat)
    keep_own(x_block)
    pl.semaphore_wait(barrier, n_e - 1 + n_c - 1)

    @pl.when(z > 0)
    def _():
        z_copy(z, -1).start()

    @pl.when(z < n_c - 1)
    def _():
        z_copy(z, 1).start()

    all_copies = {}
    all_copies[x_block] = exchange(x_block)
    for copy in all_copies[x_block]:
        copy.start()
    route(0, zbuf.at[z])
    keep_own(0)
    all_copies[0] = exchange(0)
    for copy in all_copies[0]:
        copy.start()

    def take_z(step):
        block = order[step]
        z_copy(block, 1).wait_recv()

        @pl.when((block < z) & (z < n_c - 1))
        def _():
            z_copy(block, 1).start()

        @pl.when((block > z) & (z > 0))
        def _():
            z_copy(block, -1).start()

        route(step, zbuf.at[block])
        keep_own(step)
        all_copies[step] = exchange(step)
        for copy in all_copies[step]:
            copy.start()

    def taps_at(group, cut):
        start = pl.multiple_of(group * GROUP_OUT + cut * LANES, LANES)
        return taps_ref[:, pl.ds(start, LANES)].astype(jnp.float32)

    def project(step, group):
        rows = pl.ds(pl.multiple_of(group * GROUP_OUT, GROUP_OUT), GROUP_OUT)
        return lax.dot_general(
            gbuf[step], wo[step, rows], (((1,), (1,)), ((), ())), preferred_element_type=jnp.float32
        )

    def take_block(step):
        for copy in all_copies[step]:
            copy.wait_recv()

        def store(pair, value):
            for parity in range(2):
                spot = 2 * pair + parity
                if spot < spots:
                    for tile_t in range(tiles_t):
                        gbuf[
                            step,
                            spot * slots : (spot + 1) * slots,
                            tile_t * LANES : (tile_t + 1) * LANES,
                        ] = value[parity, tile_t]

        unroute(step, store)
        wo_copies[step].wait()

    quarter = lax.broadcasted_iota(jnp.int32, (slots, LANES), 1) // (LANES // per_t)
    half = LANES // per_t

    def forward(tile_t, step):
        field = jnp.concatenate([xbuf[tile_t, spot] for spot in range(spots)], axis=0).astype(jnp.float32)
        turned = [field] + [pltpu.roll(field, half * turn, 1) for turn in range(1, per_t)]

        def part(turn, spot):
            return None if spot is None else turned[turn][spot * slots : (spot + 1) * slots]

        for inner in range(per_t):
            for spot in range(spots):
                for lane_tile in range(wc.shape[0] // LANES):
                    parts = []
                    for at in range(per_t):
                        offset = lane_tile * per_t + at
                        source = shifted(side, spot, *offs[offset]) if offset < taps_used else None
                        parts.append(part((at - inner) % per_t, source))
                    if all(item is None for item in parts):
                        value = jnp.zeros((slots, LANES), jnp.float32)
                    else:
                        value = by_quarter(quarter, parts)
                    xcol[
                        inner,
                        spot * slots : (spot + 1) * slots,
                        lane_tile * LANES : (lane_tile + 1) * LANES,
                    ] = value.astype(jnp.bfloat16)

        def each(inner, carry):
            group = tile_t * per_t + inner
            lanes = pl.ds(pl.multiple_of(group * GROUP_OUT, GROUP_OUT), GROUP_OUT)
            h_one = jnp.dot(xcol[inner], wc[:, lanes], preferred_element_type=jnp.float32)
            if step is not None:
                for part in range(tiles_t):
                    ahead = inner * tiles_t + part
                    partial[step][ahead] = project(step, ahead)
            for cut in range(GROUP_OUT // LANES):
                value = h_one[:, cut * LANES : (cut + 1) * LANES]
                cdf = 0.5 * (1.0 + lax.erf(value * 0.7071067811865476))
                slant = cdf + value * jnp.exp(-0.5 * value * value) * 0.3989422804014327
                slope[group, :, cut * LANES : (cut + 1) * LANES] = slant
                active = (value * cdf).astype(jnp.bfloat16).astype(jnp.float32)
                taps = taps_at(group, cut)
                for spot in range(spots):
                    total = None
                    for index, (row, col) in enumerate(offs):
                        source = shifted(side, spot, row, col)
                        if source is not None:
                            term = active[source * slots : (source + 1) * slots] * taps[index : index + 1]
                            total = term if total is None else total + term
                    h2[
                        group, spot * slots : (spot + 1) * slots, cut * LANES : (cut + 1) * LANES
                    ] = total.astype(jnp.bfloat16)
            return carry

        for inner in range(per_t):
            each(inner, 0)

    if n_c > 1:
        take_z(1)
    for copy in all_copies[x_block]:
        copy.wait_recv()

    def store_x(pair, value):
        for parity in range(2):
            for tile_t in range(tiles_t):
                xbuf[tile_t, 2 * pair + parity] = value[parity, tile_t]

    unroute(x_block, store_x)
    wc_copy.wait()
    early = min(len(partial), n_c - 1, tiles_t - 1)
    for tile_t in range(tiles_t):
        step = tile_t - 1 if 0 < tile_t <= early else None
        if step is not None:
            take_block(step)
        forward(tile_t, step)
        for at in range(2, n_c):
            if at - 2 == tile_t or (tile_t == tiles_t - 1 and at - 2 > tile_t):
                take_z(at)
    for step in range(early, n_c):
        take_block(step)

    gate = xbuf[0, spots].astype(jnp.float32)
    uppers = (upper_even, upper_odd)

    def finish(tile_t, carry):
        for inner in range(per_t):
            group = tile_t * per_t + inner
            product = None
            for step in range(early, n_c):
                term = project(step, group)
                product = term if product is None else product + term
            for step in range(early):
                product = product + partial[step][group]
            uppers[tile_t % 2][inner] = product
            both = product * h2[group].astype(jnp.float32)
            for spot in range(spots):
                for cut in range(GROUP_OUT // LANES):
                    carry = carry + both[
                        spot * slots : (spot + 1) * slots, cut * LANES : (cut + 1) * LANES
                    ]
        return carry

    def backward(tile_t):
        folded = []
        for inner in range(per_t):
            group = tile_t * per_t + inner
            lanes = pl.ds(pl.multiple_of(group * GROUP_OUT, GROUP_OUT), GROUP_OUT)
            sides = []
            for cut in range(GROUP_OUT // LANES):
                where = slice(cut * LANES, (cut + 1) * LANES)
                taps = taps_at(group, cut)
                d_two = [
                    (gate * uppers[tile_t % 2][inner, spot * slots : (spot + 1) * slots, where])
                    .astype(jnp.bfloat16)
                    .astype(jnp.float32)
                    for spot in range(spots)
                ]
                done = []
                for spot in range(spots):
                    total = None
                    for index, (row, col) in enumerate(offs):
                        source = shifted(side, spot, -row, -col)
                        if source is not None:
                            term = d_two[source] * taps[index : index + 1]
                            total = term if total is None else total + term
                    slant = slope[group, spot * slots : (spot + 1) * slots, where]
                    done.append((total * slant).astype(jnp.bfloat16))
                sides.append(jnp.concatenate(done, axis=0))
            d_one = jnp.concatenate(sides, axis=1)
            spread = lax.dot_general(
                d_one, wc[:, lanes], (((1,), (1,)), ((), ())), preferred_element_type=jnp.float32
            )
            sums = []
            for spot in range(spots):
                total = None
                for lane_tile in range(wc.shape[0] // LANES):
                    parts = []
                    for at in range(per_t):
                        offset = lane_tile * per_t + at
                        source = None
                        if offset < taps_used:
                            source = shifted(side, spot, -offs[offset][0], -offs[offset][1])
                        parts.append(
                            None
                            if source is None
                            else spread[
                                source * slots : (source + 1) * slots,
                                lane_tile * LANES : (lane_tile + 1) * LANES,
                            ]
                        )
                    if any(item is not None for item in parts):
                        value = by_quarter(quarter, parts)
                        total = value if total is None else total + value
                sums.append(total)
            folded.append(sums)
        for spot in range(spots):
            total = None
            for turn in range(per_t):
                value = by_quarter(
                    quarter, [folded[(at + turn) % per_t][spot] for at in range(per_t)]
                )
                value = pltpu.roll(value, half * turn, 1) if turn else value
                total = value if total is None else total + value
            dz[spot, tile_t] = total.astype(jnp.bfloat16)

    summed = finish(0, jnp.zeros((slots, LANES), jnp.float32))
    for tile_t in range(tiles_t - 1):
        summed = finish(tile_t + 1, summed)
        backward(tile_t)
    gates[z] = summed
    gate_copies = []
    for step in range(1, n_c):
        gate_copies.append(
            pltpu.make_async_remote_copy(
                src_ref=gates.at[z],
                dst_ref=gates.at[z],
                send_sem=gsend_sem.at[step],
                recv_sem=grecv_sem.at[step],
                device_id=(me, lax.rem(z + step, n_c)),
                device_id_type=MESH,
            )
        )
        gate_copies[-1].start()

    backward(tiles_t - 1)
    for copy in gate_copies:
        copy.wait_recv()
    total = gates[0]
    for at in range(1, n_c):
        total = total + gates[at]
    total = jnp.broadcast_to(jnp.sum(total, axis=1, keepdims=True), (slots, LANES))
    for tile_t in range(tiles_t):
        dz[spots, tile_t] = total.astype(jnp.bfloat16)

    for pair in range(pairs):
        field = dz[2 * pair : 2 * pair + 2].reshape(rows_routed, LANES)
        field = jnp.dot(order_back_ref[...], field, preferred_element_type=jnp.float32)
        send[back_block, :, pair] = field.astype(jnp.bfloat16).reshape(n_e, piece, LANES)
    all_copies[back_block] = exchange(back_block)
    for copy in all_copies[back_block]:
        copy.start()
    own_copy = pltpu.make_async_copy(send.at[back_block, me], back_ref.at[me], own_sem)
    own_copy.start()
    for copy in all_copies[back_block]:
        copy.wait_recv()
    own_copy.wait()

    for block in all_copies:
        for copy in all_copies[block]:
            copy.wait_send()
    for copy in gate_copies:
        copy.wait_send()

    @pl.when(z > 0)
    def _():
        z_copy(z, -1).wait_send()

    @pl.when(z < n_c - 1)
    def _():
        z_copy(z, 1).wait_send()

    for step in range(1, n_c):
        block = order[step]

        @pl.when((block < z) & (z < n_c - 1))
        def _():
            z_copy(block, 1).wait_send()

        @pl.when((block > z) & (z > 0))
        def _():
            z_copy(block, -1).wait_send()


def on_device(tiles_in, grad_out, gate, expert_id, w_conv, w_depth, w_out):
    owned, side, local_feat = tiles_in.shape[0], tiles_in.shape[1], tiles_in.shape[3]
    n_e, n_c = lax.axis_size("expert"), lax.axis_size("chan")
    hidden = w_out.shape[1]
    tiles_t = local_feat // LANES
    spots = side * side
    pairs = (spots + 1) // 2
    slots = n_e * CAP
    piece = 2 * CAP * tiles_t
    groups = hidden // GROUP_OUT
    group_in = w_conv.shape[3]
    rows_here, rows_routed = 2 * owned * tiles_t, n_e * piece

    column = np.arange(rows_here)
    lane_t, parity, tile = column // (2 * owned), column // owned % 2, column % owned
    base = (tile << 16) + parity * CAP * tiles_t + lane_t
    base_row = jnp.asarray(base.reshape(1, -1), jnp.int32)
    base_col = jnp.asarray(base.reshape(-1, 1), jnp.int32)
    row = np.arange(rows_routed)
    parity, lane_t = row // (tiles_t * slots), row // slots % tiles_t
    source, rank = row % slots // CAP, row % CAP
    order = np.zeros((rows_routed, rows_routed), np.float32)
    order[row, ((source * 2 + parity) * CAP + rank) * tiles_t + lane_t] = 1.0
    taps_rows = 9 * group_in
    padded_rows = -(-taps_rows // LANES) * LANES
    dims = (n_e, n_c, owned, tiles_t, side)
    vmem = pl.BlockSpec(memory_space=pltpu.VMEM)
    anywhere = pl.BlockSpec(memory_space=pl.ANY)
    blocks = n_c + 2
    bf16, f32 = jnp.bfloat16, jnp.float32
    ids = expert_id.reshape(owned)
    back = pl.pallas_call(
        functools.partial(expert_kernel, dims),
        out_shape=jax.ShapeDtypeStruct((n_e, pairs, piece, LANES), bf16),
        in_specs=[pl.BlockSpec(memory_space=pltpu.SMEM)] + [vmem] * 7 + [anywhere] * 2,
        out_specs=anywhere,
        scratch_shapes=[
            pltpu.VMEM((padded_rows, hidden), bf16),
            pltpu.VMEM((n_c, hidden, local_feat), bf16),
            pltpu.VMEM((2 * pairs * owned, local_feat), bf16),
            pltpu.VMEM((n_c, 2 * pairs * owned, local_feat), bf16),
            pltpu.VMEM((blocks, n_e, pairs, piece, LANES), bf16),
            pltpu.VMEM((blocks - 1, n_e, pairs, piece, LANES), bf16),
            pltpu.VMEM((tiles_t, 2 * pairs, slots, LANES), bf16),
            pltpu.VMEM((n_c, spots * slots, local_feat), bf16),
            pltpu.VMEM((LANES // group_in, spots * slots, padded_rows), bf16),
            pltpu.VMEM((groups, spots * slots, GROUP_OUT), bf16),
            pltpu.VMEM((groups, spots * slots, GROUP_OUT), f32),
            pltpu.VMEM((groups, spots * slots, GROUP_OUT), f32),
            pltpu.VMEM((groups, spots * slots, GROUP_OUT), f32),
            pltpu.VMEM((groups, spots * slots, GROUP_OUT), f32),
            pltpu.VMEM((groups // tiles_t, spots * slots, GROUP_OUT), f32),
            pltpu.VMEM((groups // tiles_t, spots * slots, GROUP_OUT), f32),
            pltpu.VMEM((2 * pairs, tiles_t, slots, LANES), bf16),
            pltpu.VMEM((n_c, slots, LANES), f32),
            pltpu.SemaphoreType.DMA,
            pltpu.SemaphoreType.DMA((n_c,)),
            pltpu.SemaphoreType.DMA((n_c, 2)),
            pltpu.SemaphoreType.DMA((n_c,)),
            pltpu.SemaphoreType.DMA((blocks, n_e)),
            pltpu.SemaphoreType.DMA((blocks, n_e)),
            pltpu.SemaphoreType.DMA((n_c,)),
            pltpu.SemaphoreType.DMA((n_c,)),
            pltpu.SemaphoreType.DMA,
        ],
        compiler_params=pltpu.CompilerParams(
            collective_id=0, has_side_effects=True, vmem_limit_bytes=56 * 1024 * 1024
        ),
    )(
        ids,
        tiles_in.transpose(1, 2, 0, 3).reshape(spots * owned, local_feat),
        grad_out.transpose(1, 2, 0, 3).reshape(spots * owned, local_feat),
        gate.reshape(1, owned),
        base_row,
        jnp.asarray(order, bf16),
        jnp.asarray(order.T, bf16),
        w_depth.reshape(9, hidden),
        w_conv.reshape(taps_rows, hidden),
        w_out.reshape(hidden, w_out.shape[2]),
    )
    grad_input, grad_gate = pl.pallas_call(
        functools.partial(owner_kernel, dims),
        out_shape=(
            jax.ShapeDtypeStruct((spots * owned, local_feat), bf16),
            jax.ShapeDtypeStruct((owned,), bf16),
        ),
        in_specs=[pl.BlockSpec(memory_space=pltpu.SMEM), vmem, vmem],
        out_specs=(vmem, vmem),
    )(ids, base_col, back)
    grad_input = grad_input.reshape(side, side, owned, local_feat).transpose(2, 0, 1, 3)
    return grad_input, grad_gate


def choose(tiles_in, grad_out, gate, expert_id, w_conv, w_depth, w_out):
    owned, side, local_feat = tiles_in.shape[0], tiles_in.shape[1], tiles_in.shape[3]
    count = local_feat // w_conv.shape[3]
    whole = local_feat % LANES == 0 and 2 * CAP * (local_feat // LANES) % 16 == 0
    whole = whole and lax.axis_size("expert") * CAP % 16 == 0 and side % 2 == 1 and owned % 8 == 0
    whole = whole and w_out.shape[1] == count * GROUP_OUT and LANES % w_conv.shape[3] == 0
    body = on_device if whole else on_device_plain
    return body(tiles_in, grad_out, gate, expert_id, w_conv, w_depth, w_out)


def solution(mesh):
    in_specs = (
        P("expert", None, None, "chan"),
        P("expert", None, None, "chan"),
        P("expert"),
        P("expert", None),
        P("expert", None, None, None, "chan"),
        P("expert", None, "chan"),
        P("expert", "chan", None),
    )
    out_specs = (P("expert", None, None, "chan"), P("expert"))
    return jax.shard_map(
        choose, mesh=mesh, in_specs=in_specs, out_specs=out_specs, check_vma=False
    )
```

```python
import functools
import jax
import jax.numpy as jnp
import numpy as np
from jax import lax
from jax.experimental import pallas as pl
from jax.experimental.pallas import tpu as pltpu
from jax.sharding import PartitionSpec as P

CAP = 2


def group_conv(field, kernel, count):
    return lax.conv_general_dilated(
        field,
        kernel,
        (1, 1),
        "SAME",
        dimension_numbers=("NHWC", "HWIO", "NHWC"),
        feature_group_count=count,
        preferred_element_type=jnp.float32,
    )


def conv_back(field, kernel, count, cotangent):
    forward_value, pullback = jax.vjp(lambda value: group_conv(value, kernel, count), field)
    return pullback(cotangent)[0]


def gelu_slope(value):
    normal_cdf = 0.5 * (1.0 + jax.scipy.special.erf(value * 0.7071067811865476))
    return normal_cdf + value * jnp.exp(-0.5 * value * value) * 0.3989422804014327


def depth_forward(field, taps):
    side = field.shape[1]
    padded = jnp.pad(field, ((0, 0), (1, 1), (1, 1), (0, 0))).astype(jnp.float32)
    total = jnp.zeros(field.shape, jnp.float32)
    for row_off in range(3):
        for col_off in range(3):
            total = total + padded[:, row_off : row_off + side, col_off : col_off + side, :] * taps[
                3 * row_off + col_off
            ].astype(jnp.float32)
    return total


def depth_back(field, taps):
    side = field.shape[1]
    padded = jnp.pad(field, ((0, 0), (1, 1), (1, 1), (0, 0))).astype(jnp.float32)
    total = jnp.zeros(field.shape, jnp.float32)
    for row_off in range(3):
        for col_off in range(3):
            total = total + padded[
                :, 2 - row_off : 2 - row_off + side, 2 - col_off : 2 - col_off + side, :
            ] * taps[3 * row_off + col_off].astype(jnp.float32)
    return total


def on_device_plain(tiles_in, grad_out, gate, expert_id, w_conv, w_depth, w_out):
    owned, side = (tiles_in.shape[0], tiles_in.shape[1])
    local_feat = tiles_in.shape[3]
    sections = lax.axis_size("expert")
    capacity = CAP
    slots = sections * capacity
    chosen = expert_id[:, 0]
    matches = (chosen[:, None] == jnp.arange(sections, dtype=jnp.int32)[None, :]).astype(jnp.int32)
    rows_idx = jnp.arange(owned, dtype=jnp.int32)
    earlier = (rows_idx[:, None] > rows_idx[None, :]).astype(jnp.int32)
    before = jnp.dot(earlier, matches)
    rank = jnp.sum(before * matches, axis=1)
    slot = chosen * capacity + rank
    placing = (slot[:, None] == jnp.arange(slots, dtype=jnp.int32)[None, :]).astype(jnp.bfloat16)
    flat = jnp.concatenate([tiles_in.reshape(owned, -1), grad_out.reshape(owned, -1)], axis=1)
    outward = lax.dot_general(
        placing, flat, (((0,), (0,)), ((), ())), preferred_element_type=jnp.float32
    ).astype(jnp.bfloat16)
    gate_out = lax.dot_general(
        placing,
        gate.reshape(owned, 1),
        (((0,), (0,)), ((), ())),
        preferred_element_type=jnp.float32,
    ).astype(jnp.bfloat16)
    arrived, gate_in = (
        lax.all_to_all(
            outward.reshape(sections, capacity, -1),
            "expert",
            split_axis=0,
            concat_axis=0,
            tiled=True,
        ),
        lax.all_to_all(
            gate_out.reshape(sections, capacity), "expert", split_axis=0, concat_axis=0, tiled=True
        ),
    )
    width = side * side * local_feat
    arrived = arrived.reshape(slots, 2 * width)
    inputs = arrived[:, :width].reshape(slots, side, side, local_feat)
    grads = arrived[:, width:].reshape(slots, side, side, local_feat)
    gates = gate_in.reshape(slots).astype(jnp.float32)
    kernel = w_conv[0]
    taps = w_depth[0]
    project = w_out[0]
    hidden = project.shape[0]
    count = local_feat // kernel.shape[2]
    h_one = group_conv(inputs, kernel, count)
    active = jax.nn.gelu(h_one, approximate=False).astype(jnp.bfloat16)
    h_two = depth_forward(active, taps).astype(jnp.bfloat16)
    gathered = lax.all_gather(grads, "chan", axis=3, tiled=True)
    upper = lax.dot_general(
        gathered.reshape(slots * side * side, -1),
        project,
        (((1,), (1,)), ((), ())),
        preferred_element_type=jnp.float32,
    )
    upper = upper.reshape(slots, side, side, hidden)
    partial_grad = jnp.sum(h_two.astype(jnp.float32) * upper, axis=(1, 2, 3))
    gate_grad = lax.psum(partial_grad, "chan").astype(jnp.bfloat16)
    d_two = (gates[:, None, None, None] * upper).astype(jnp.bfloat16)
    d_act = depth_back(d_two, taps)
    d_one = (d_act * gelu_slope(h_one)).astype(jnp.bfloat16)
    d_input = conv_back(inputs, kernel, count, d_one.astype(jnp.float32))
    back_rows, back_gate = (
        lax.all_to_all(
            d_input.reshape(sections, capacity, -1),
            "expert",
            split_axis=0,
            concat_axis=0,
            tiled=True,
        ),
        lax.all_to_all(
            gate_grad.reshape(sections, capacity), "expert", split_axis=0, concat_axis=0, tiled=True
        ),
    )
    grad_input = jnp.dot(
        placing, back_rows.reshape(slots, -1), preferred_element_type=jnp.float32
    ).astype(jnp.bfloat16)
    grad_gate = jnp.dot(
        placing, back_gate.reshape(slots, 1), preferred_element_type=jnp.float32
    ).astype(jnp.bfloat16)
    return (grad_input.reshape(owned, side, side, local_feat), grad_gate.reshape(owned))


LANES = 128
GROUP_OUT = 256
MESH = pl.DeviceIdType.MESH


def offsets(side):
    found = []
    for row in range(-1, 2):
        for col in range(-1, 2):
            found.append((row, col))
    return found


def shifted(side, position, row, col):
    at_row, at_col = position // side + row, position % side + col
    if 0 <= at_row < side and 0 <= at_col < side:
        return at_row * side + at_col
    return None


def by_quarter(quarter, parts):
    shape = next(part for part in parts if part is not None).shape
    total = None
    for index, part in enumerate(parts):
        part = jnp.zeros(shape, jnp.float32) if part is None else part
        total = part if total is None else jnp.where(quarter == index, part, total)
    return total


def slot_codes(ids_ref, owned, piece, tiles_t):
    names = [ids_ref[tile] for tile in range(owned)]
    codes = []
    for tile in range(owned):
        rank = jnp.int32(0)
        for earlier in range(tile):
            rank = rank + jnp.where(names[earlier] == names[tile], 1, 0)
        codes.append(names[tile] * piece + rank * tiles_t)
    return codes


def target(base, codes):
    total = base & 0xFFFF
    at_tile = base >> 16
    for tile, code in enumerate(codes):
        total = total + jnp.where(at_tile == tile, code, 0)
    return total


def owner_kernel(dims, ids_ref, base_col_ref, back_ref, out_ref, gate_out_ref):
    n_e, n_c, owned, tiles_t, side = dims
    spots = side * side
    pairs = (spots + 1) // 2
    piece = 2 * CAP * tiles_t
    strip = 2 * owned
    rows_here, rows_routed = 2 * owned * tiles_t, n_e * piece
    codes = slot_codes(ids_ref, owned, piece, tiles_t)
    place_back = jnp.where(
        lax.broadcasted_iota(jnp.int32, (rows_here, rows_routed), 1)
        == target(base_col_ref[...], codes),
        1.0,
        0.0,
    ).astype(jnp.bfloat16)
    for pair in range(pairs):
        got = back_ref[:, pair].reshape(rows_routed, LANES)
        got = jnp.dot(place_back, got, preferred_element_type=jnp.float32)
        got = jnp.concatenate([got[at * strip : (at + 1) * strip] for at in range(tiles_t)], axis=1)
        if pair < pairs - 1:
            out_ref[pair * strip : (pair + 1) * strip] = got.astype(jnp.bfloat16)
        else:
            out_ref[pair * strip :] = got[:owned].astype(jnp.bfloat16)
            rows = got[owned:, :owned]
    diagonal = lax.broadcasted_iota(jnp.int32, (owned, owned), 0) == lax.broadcasted_iota(
        jnp.int32, (owned, owned), 1
    )
    gate_row = jnp.sum(jnp.where(diagonal, rows, 0.0), axis=0, keepdims=True)
    gate_out_ref[...] = gate_row.astype(jnp.bfloat16).reshape(gate_out_ref.shape)


def expert_kernel(
    dims,
    ids_ref,
    x_ref,
    g_ref,
    gate_ref,
    base_row_ref,
    order_ref,
    order_back_ref,
    taps_ref,
    wc_hbm,
    wo_hbm,
    back_ref,
    wc,
    wo,
    flat,
    zbuf,
    send,
    recv,
    xbuf,
    gbuf,
    xcol,
    h2,
    slope,
    partial_first,
    partial_second,
    partial_third,
    upper_even,
    upper_odd,
    dz,
    gates,
    wc_sem,
    wo_sem,
    zsend_sem,
    zrecv_sem,
    send_sem,
    recv_sem,
    gsend_sem,
    grecv_sem,
    own_sem,
):
    n_e, n_c, owned, tiles_t, side = dims
    spots = side * side
    pairs = (spots + 1) // 2
    slots = n_e * CAP
    groups = wc.shape[1] // GROUP_OUT
    per_t = groups // tiles_t
    width = tiles_t * LANES
    piece = 2 * CAP * tiles_t
    me, z = lax.axis_index("expert"), lax.axis_index("chan")
    partial = (partial_first, partial_second, partial_third)
    offs = offsets(side)
    taps_used = len(offs)

    order = []
    for step in range(n_c):
        block = 0
        for at in range(n_c):
            ranked = sorted(range(n_c), key=lambda other: (abs(other - at), other if 2 * at < n_c else -other))
            block = block + jnp.where(z == at, ranked[step], 0)
        order.append(block)

    wc_copy = pltpu.make_async_copy(wc_hbm, wc.at[pl.ds(0, wc_hbm.shape[0])], wc_sem)
    wc_copy.start()
    wo_copies = []
    for step in range(n_c):
        start = pl.multiple_of(order[step] * width, width)
        wo_copies.append(
            pltpu.make_async_copy(wo_hbm.at[:, pl.ds(start, width)], wo.at[step], wo_sem.at[step])
        )
        wo_copies[step].start()

    barrier = pltpu.get_barrier_semaphore()
    for step in range(1, n_e):
        pl.semaphore_signal(
            barrier, inc=1, device_id=(lax.rem(me + step, n_e), z), device_id_type=MESH
        )
    for step in range(1, n_c):
        pl.semaphore_signal(
            barrier, inc=1, device_id=(me, lax.rem(z + step, n_c)), device_id_type=MESH
        )

    wc[pl.ds(wc_hbm.shape[0], wc.shape[0] - wc_hbm.shape[0])] = jnp.zeros(
        (wc.shape[0] - wc_hbm.shape[0], wc.shape[1]), jnp.bfloat16
    )

    codes = slot_codes(ids_ref, owned, piece, tiles_t)
    rows_here, rows_routed = 2 * owned * tiles_t, n_e * piece

    place = jnp.where(
        lax.broadcasted_iota(jnp.int32, (rows_routed, rows_here), 0) == target(base_row_ref[...], codes),
        1.0,
        0.0,
    ).astype(jnp.bfloat16)

    strip = 2 * owned

    def route(block, field):
        for pair in range(pairs):
            taken = field[pair * strip : (pair + 1) * strip, :]
            taken = jnp.concatenate(
                [taken[:, at * LANES : (at + 1) * LANES] for at in range(tiles_t)], axis=0
            )
            routed = jnp.dot(place, taken, preferred_element_type=jnp.float32)
            send[block, :, pair] = routed.astype(jnp.bfloat16).reshape(n_e, piece, LANES)

    def exchange(block):
        copies = []
        for step in range(1, n_e):
            peer = lax.rem(me + step, n_e)
            copies.append(
                pltpu.make_async_remote_copy(
                    src_ref=send.at[block, peer],
                    dst_ref=back_ref.at[me] if block == back_block else recv.at[block, me],
                    send_sem=send_sem.at[block, step],
                    recv_sem=recv_sem.at[block, step],
                    device_id=(peer, z),
                    device_id_type=MESH,
                )
            )
        return copies

    def keep_own(block):
        recv[block, me] = send[block, me]

    def unroute(block, store):
        for pair in range(pairs):
            got = recv[block, :, pair].reshape(rows_routed, LANES)
            got = jnp.dot(order_ref[...], got, preferred_element_type=jnp.float32)
            store(pair, got.astype(jnp.bfloat16).reshape(2, tiles_t, slots, LANES))

    def z_copy(block, toward):
        return pltpu.make_async_remote_copy(
            src_ref=zbuf.at[block],
            dst_ref=zbuf.at[block],
            send_sem=zsend_sem.at[block, (toward + 1) // 2],
            recv_sem=zrecv_sem.at[block],
            device_id=(me, z + toward),
            device_id_type=MESH,
        )

    x_block = n_c
    back_block = n_c + 1
    zbuf[z] = jnp.concatenate(
        [g_ref[...].astype(jnp.float32), jnp.zeros((owned, width), jnp.float32)], axis=0
    ).astype(jnp.bfloat16)
    diagonal = lax.broadcasted_iota(jnp.int32, (owned, owned), 0) == lax.broadcasted_iota(
        jnp.int32, (owned, owned), 1
    )
    spread_gate = jnp.where(diagonal, gate_ref[...].astype(jnp.float32), 0.0)
    spread_gate = jnp.broadcast_to(jnp.sum(spread_gate, axis=1, keepdims=True), (owned, width))
    flat[...] = jnp.concatenate(
        [x_ref[...].astype(jnp.float32), spread_gate], axis=0
    ).astype(jnp.bfloat16)
    route(x_block, flat)
    keep_own(x_block)
    route(0, zbuf.at[z])
    keep_own(0)
    pl.semaphore_wait(barrier, n_e - 1 + n_c - 1)

    @pl.when(z > 0)
    def _():
        z_copy(z, -1).start()

    @pl.when(z < n_c - 1)
    def _():
        z_copy(z, 1).start()

    all_copies = {}
    all_copies[x_block] = exchange(x_block)
    for copy in all_copies[x_block]:
        copy.start()
    all_copies[0] = exchange(0)
    for copy in all_copies[0]:
        copy.start()

    def take_z(step):
        block = order[step]
        z_copy(block, 1).wait_recv()

        @pl.when((block < z) & (z < n_c - 1))
        def _():
            z_copy(block, 1).start()

        @pl.when((block > z) & (z > 0))
        def _():
            z_copy(block, -1).start()

        route(step, zbuf.at[block])
        all_copies[step] = exchange(step)
        for copy in all_copies[step]:
            copy.start()
        keep_own(step)

    def taps_at(group, cut):
        start = pl.multiple_of(group * GROUP_OUT + cut * LANES, LANES)
        return taps_ref[:, pl.ds(start, LANES)].astype(jnp.float32)

    def project(step, group):
        rows = pl.ds(pl.multiple_of(group * GROUP_OUT, GROUP_OUT), GROUP_OUT)
        return lax.dot_general(
            gbuf[step], wo[step, rows], (((1,), (1,)), ((), ())), preferred_element_type=jnp.float32
        )

    def take_block(step):
        for copy in all_copies[step]:
            copy.wait_recv()

        def store(pair, value):
            for parity in range(2):
                spot = 2 * pair + parity
                if spot < spots:
                    for tile_t in range(tiles_t):
                        gbuf[
                            step,
                            spot * slots : (spot + 1) * slots,
                            tile_t * LANES : (tile_t + 1) * LANES,
                        ] = value[parity, tile_t]

        unroute(step, store)
        wo_copies[step].wait()

    quarter = lax.broadcasted_iota(jnp.int32, (slots, LANES), 1) // (LANES // per_t)
    half = LANES // per_t

    def forward(tile_t, step):
        field = jnp.concatenate([xbuf[tile_t, spot] for spot in range(spots)], axis=0).astype(jnp.float32)
        turned = [field] + [pltpu.roll(field, half * turn, 1) for turn in range(1, per_t)]

        def part(turn, spot):
            return None if spot is None else turned[turn][spot * slots : (spot + 1) * slots]

        for inner in range(per_t):
            for spot in range(spots):
                for lane_tile in range(wc.shape[0] // LANES):
                    parts = []
                    for at in range(per_t):
                        offset = lane_tile * per_t + at
                        source = shifted(side, spot, *offs[offset]) if offset < taps_used else None
                        parts.append(part((at - inner) % per_t, source))
                    if all(item is None for item in parts):
                        value = jnp.zeros((slots, LANES), jnp.float32)
                    else:
                        value = by_quarter(quarter, parts)
                    xcol[
                        inner,
                        spot * slots : (spot + 1) * slots,
                        lane_tile * LANES : (lane_tile + 1) * LANES,
                    ] = value.astype(jnp.bfloat16)

        def each(inner, carry):
            group = tile_t * per_t + inner
            lanes = pl.ds(pl.multiple_of(group * GROUP_OUT, GROUP_OUT), GROUP_OUT)
            h_one = jnp.dot(xcol[inner], wc[:, lanes], preferred_element_type=jnp.float32)
            if step is not None:
                for part in range(tiles_t):
                    ahead = inner * tiles_t + part
                    partial[step][ahead] = project(step, ahead)
            for cut in range(GROUP_OUT // LANES):
                value = h_one[:, cut * LANES : (cut + 1) * LANES]
                cdf = 0.5 * (1.0 + lax.erf(value * 0.7071067811865476))
                slant = cdf + value * jnp.exp(-0.5 * value * value) * 0.3989422804014327
                slope[group, :, cut * LANES : (cut + 1) * LANES] = slant
                active = (value * cdf).astype(jnp.bfloat16).astype(jnp.float32)
                taps = taps_at(group, cut)
                for spot in range(spots):
                    total = None
                    for index, (row, col) in enumerate(offs):
                        source = shifted(side, spot, row, col)
                        if source is not None:
                            term = active[source * slots : (source + 1) * slots] * taps[index : index + 1]
                            total = term if total is None else total + term
                    h2[
                        group, spot * slots : (spot + 1) * slots, cut * LANES : (cut + 1) * LANES
                    ] = total.astype(jnp.bfloat16)
            return carry

        for inner in range(per_t):
            each(inner, 0)

    if n_c > 1:
        take_z(1)
    for copy in all_copies[x_block]:
        copy.wait_recv()

    def store_x(pair, value):
        for parity in range(2):
            for tile_t in range(tiles_t):
                xbuf[tile_t, 2 * pair + parity] = value[parity, tile_t]

    unroute(x_block, store_x)
    wc_copy.wait()
    early = min(len(partial), n_c - 1, tiles_t - 1)
    for tile_t in range(tiles_t):
        step = tile_t - 1 if 0 < tile_t <= early else None
        if step is not None:
            take_block(step)
        forward(tile_t, step)
        for at in range(2, n_c):
            if at - 2 == tile_t or (tile_t == tiles_t - 1 and at - 2 > tile_t):
                take_z(at)
    for step in range(early, n_c):
        take_block(step)

    gate = xbuf[0, spots].astype(jnp.float32)
    uppers = (upper_even, upper_odd)

    def finish(tile_t, carry):
        for inner in range(per_t):
            group = tile_t * per_t + inner
            product = None
            for step in range(early, n_c):
                term = project(step, group)
                product = term if product is None else product + term
            for step in range(early):
                product = product + partial[step][group]
            uppers[tile_t % 2][inner] = product
            both = product * h2[group].astype(jnp.float32)
            for spot in range(spots):
                for cut in range(GROUP_OUT // LANES):
                    carry = carry + both[
                        spot * slots : (spot + 1) * slots, cut * LANES : (cut + 1) * LANES
                    ]
        return carry

    def backward(tile_t):
        folded = []
        for inner in range(per_t):
            group = tile_t * per_t + inner
            lanes = pl.ds(pl.multiple_of(group * GROUP_OUT, GROUP_OUT), GROUP_OUT)
            sides = []
            for cut in range(GROUP_OUT // LANES):
                where = slice(cut * LANES, (cut + 1) * LANES)
                taps = taps_at(group, cut)
                d_two = [
                    (gate * uppers[tile_t % 2][inner, spot * slots : (spot + 1) * slots, where])
                    .astype(jnp.bfloat16)
                    .astype(jnp.float32)
                    for spot in range(spots)
                ]
                done = []
                for spot in range(spots):
                    total = None
                    for index, (row, col) in enumerate(offs):
                        source = shifted(side, spot, -row, -col)
                        if source is not None:
                            term = d_two[source] * taps[index : index + 1]
                            total = term if total is None else total + term
                    slant = slope[group, spot * slots : (spot + 1) * slots, where]
                    done.append((total * slant).astype(jnp.bfloat16))
                sides.append(jnp.concatenate(done, axis=0))
            d_one = jnp.concatenate(sides, axis=1)
            spread = lax.dot_general(
                d_one, wc[:, lanes], (((1,), (1,)), ((), ())), preferred_element_type=jnp.float32
            )
            sums = []
            for spot in range(spots):
                total = None
                for lane_tile in range(wc.shape[0] // LANES):
                    parts = []
                    for at in range(per_t):
                        offset = lane_tile * per_t + at
                        source = None
                        if offset < taps_used:
                            source = shifted(side, spot, -offs[offset][0], -offs[offset][1])
                        parts.append(
                            None
                            if source is None
                            else spread[
                                source * slots : (source + 1) * slots,
                                lane_tile * LANES : (lane_tile + 1) * LANES,
                            ]
                        )
                    if any(item is not None for item in parts):
                        value = by_quarter(quarter, parts)
                        total = value if total is None else total + value
                sums.append(total)
            folded.append(sums)
        for spot in range(spots):
            total = None
            for turn in range(per_t):
                value = by_quarter(
                    quarter, [folded[(at + turn) % per_t][spot] for at in range(per_t)]
                )
                value = pltpu.roll(value, half * turn, 1) if turn else value
                total = value if total is None else total + value
            dz[spot, tile_t] = total.astype(jnp.bfloat16)

    summed = finish(0, jnp.zeros((slots, LANES), jnp.float32))
    for tile_t in range(tiles_t - 1):
        summed = finish(tile_t + 1, summed)
        backward(tile_t)
    gates[z] = summed
    gate_copies = []
    for step in range(1, n_c):
        gate_copies.append(
            pltpu.make_async_remote_copy(
                src_ref=gates.at[z],
                dst_ref=gates.at[z],
                send_sem=gsend_sem.at[step],
                recv_sem=grecv_sem.at[step],
                device_id=(me, lax.rem(z + step, n_c)),
                device_id_type=MESH,
            )
        )
        gate_copies[-1].start()

    backward(tiles_t - 1)
    for copy in gate_copies:
        copy.wait_recv()
    total = gates[0]
    for at in range(1, n_c):
        total = total + gates[at]
    total = jnp.broadcast_to(jnp.sum(total, axis=1, keepdims=True), (slots, LANES))
    for tile_t in range(tiles_t):
        dz[spots, tile_t] = total.astype(jnp.bfloat16)

    for pair in range(pairs):
        field = dz[2 * pair : 2 * pair + 2].reshape(rows_routed, LANES)
        field = jnp.dot(order_back_ref[...], field, preferred_element_type=jnp.float32)
        send[back_block, :, pair] = field.astype(jnp.bfloat16).reshape(n_e, piece, LANES)
    all_copies[back_block] = exchange(back_block)
    for copy in all_copies[back_block]:
        copy.start()
    own_copy = pltpu.make_async_copy(send.at[back_block, me], back_ref.at[me], own_sem)
    own_copy.start()
    for copy in all_copies[back_block]:
        copy.wait_recv()
    own_copy.wait()

    for block in all_copies:
        for copy in all_copies[block]:
            copy.wait_send()
    for copy in gate_copies:
        copy.wait_send()

    @pl.when(z > 0)
    def _():
        z_copy(z, -1).wait_send()

    @pl.when(z < n_c - 1)
    def _():
        z_copy(z, 1).wait_send()

    for step in range(1, n_c):
        block = order[step]

        @pl.when((block < z) & (z < n_c - 1))
        def _():
            z_copy(block, 1).wait_send()

        @pl.when((block > z) & (z > 0))
        def _():
            z_copy(block, -1).wait_send()


def on_device(tiles_in, grad_out, gate, expert_id, w_conv, w_depth, w_out):
    owned, side, local_feat = tiles_in.shape[0], tiles_in.shape[1], tiles_in.shape[3]
    n_e, n_c = lax.axis_size("expert"), lax.axis_size("chan")
    hidden = w_out.shape[1]
    tiles_t = local_feat // LANES
    spots = side * side
    pairs = (spots + 1) // 2
    slots = n_e * CAP
    piece = 2 * CAP * tiles_t
    groups = hidden // GROUP_OUT
    group_in = w_conv.shape[3]
    rows_here, rows_routed = 2 * owned * tiles_t, n_e * piece

    column = np.arange(rows_here)
    lane_t, parity, tile = column // (2 * owned), column // owned % 2, column % owned
    base = (tile << 16) + parity * CAP * tiles_t + lane_t
    base_row = jnp.asarray(base.reshape(1, -1), jnp.int32)
    base_col = jnp.asarray(base.reshape(-1, 1), jnp.int32)
    row = np.arange(rows_routed)
    parity, lane_t = row // (tiles_t * slots), row // slots % tiles_t
    source, rank = row % slots // CAP, row % CAP
    order = np.zeros((rows_routed, rows_routed), np.float32)
    order[row, ((source * 2 + parity) * CAP + rank) * tiles_t + lane_t] = 1.0
    taps_rows = 9 * group_in
    padded_rows = -(-taps_rows // LANES) * LANES
    dims = (n_e, n_c, owned, tiles_t, side)
    vmem = pl.BlockSpec(memory_space=pltpu.VMEM)
    anywhere = pl.BlockSpec(memory_space=pl.ANY)
    blocks = n_c + 2
    bf16, f32 = jnp.bfloat16, jnp.float32
    ids = expert_id.reshape(owned)
    back = pl.pallas_call(
        functools.partial(expert_kernel, dims),
        out_shape=jax.ShapeDtypeStruct((n_e, pairs, piece, LANES), bf16),
        in_specs=[pl.BlockSpec(memory_space=pltpu.SMEM)] + [vmem] * 7 + [anywhere] * 2,
        out_specs=anywhere,
        scratch_shapes=[
            pltpu.VMEM((padded_rows, hidden), bf16),
            pltpu.VMEM((n_c, hidden, local_feat), bf16),
            pltpu.VMEM((2 * pairs * owned, local_feat), bf16),
            pltpu.VMEM((n_c, 2 * pairs * owned, local_feat), bf16),
            pltpu.VMEM((blocks, n_e, pairs, piece, LANES), bf16),
            pltpu.VMEM((blocks - 1, n_e, pairs, piece, LANES), bf16),
            pltpu.VMEM((tiles_t, 2 * pairs, slots, LANES), bf16),
            pltpu.VMEM((n_c, spots * slots, local_feat), bf16),
            pltpu.VMEM((LANES // group_in, spots * slots, padded_rows), bf16),
            pltpu.VMEM((groups, spots * slots, GROUP_OUT), bf16),
            pltpu.VMEM((groups, spots * slots, GROUP_OUT), f32),
            pltpu.VMEM((groups, spots * slots, GROUP_OUT), f32),
            pltpu.VMEM((groups, spots * slots, GROUP_OUT), f32),
            pltpu.VMEM((groups, spots * slots, GROUP_OUT), f32),
            pltpu.VMEM((groups // tiles_t, spots * slots, GROUP_OUT), f32),
            pltpu.VMEM((groups // tiles_t, spots * slots, GROUP_OUT), f32),
            pltpu.VMEM((2 * pairs, tiles_t, slots, LANES), bf16),
            pltpu.VMEM((n_c, slots, LANES), f32),
            pltpu.SemaphoreType.DMA,
            pltpu.SemaphoreType.DMA((n_c,)),
            pltpu.SemaphoreType.DMA((n_c, 2)),
            pltpu.SemaphoreType.DMA((n_c,)),
            pltpu.SemaphoreType.DMA((blocks, n_e)),
            pltpu.SemaphoreType.DMA((blocks, n_e)),
            pltpu.SemaphoreType.DMA((n_c,)),
            pltpu.SemaphoreType.DMA((n_c,)),
            pltpu.SemaphoreType.DMA,
        ],
        compiler_params=pltpu.CompilerParams(
            collective_id=0, has_side_effects=True, vmem_limit_bytes=56 * 1024 * 1024
        ),
    )(
        ids,
        tiles_in.transpose(1, 2, 0, 3).reshape(spots * owned, local_feat),
        grad_out.transpose(1, 2, 0, 3).reshape(spots * owned, local_feat),
        gate.reshape(1, owned),
        base_row,
        jnp.asarray(order, bf16),
        jnp.asarray(order.T, bf16),
        w_depth.reshape(9, hidden),
        w_conv.reshape(taps_rows, hidden),
        w_out.reshape(hidden, w_out.shape[2]),
    )
    grad_input, grad_gate = pl.pallas_call(
        functools.partial(owner_kernel, dims),
        out_shape=(
            jax.ShapeDtypeStruct((spots * owned, local_feat), bf16),
            jax.ShapeDtypeStruct((owned,), bf16),
        ),
        in_specs=[pl.BlockSpec(memory_space=pltpu.SMEM), vmem, vmem],
        out_specs=(vmem, vmem),
    )(ids, base_col, back)
    grad_input = grad_input.reshape(side, side, owned, local_feat).transpose(2, 0, 1, 3)
    return grad_input, grad_gate


def choose(tiles_in, grad_out, gate, expert_id, w_conv, w_depth, w_out):
    owned, side, local_feat = tiles_in.shape[0], tiles_in.shape[1], tiles_in.shape[3]
    count = local_feat // w_conv.shape[3]
    whole = local_feat % LANES == 0 and 2 * CAP * (local_feat // LANES) % 16 == 0
    whole = whole and lax.axis_size("expert") * CAP % 16 == 0 and side % 2 == 1 and owned % 8 == 0
    whole = whole and w_out.shape[1] == count * GROUP_OUT and LANES % w_conv.shape[3] == 0
    body = on_device if whole else on_device_plain
    return body(tiles_in, grad_out, gate, expert_id, w_conv, w_depth, w_out)


def solution(mesh):
    in_specs = (
        P("expert", None, None, "chan"),
        P("expert", None, None, "chan"),
        P("expert"),
        P("expert", None),
        P("expert", None, None, None, "chan"),
        P("expert", None, "chan"),
        P("expert", "chan", None),
    )
    out_specs = (P("expert", None, None, "chan"), P("expert"))
    return jax.shard_map(
        choose, mesh=mesh, in_specs=in_specs, out_specs=out_specs, check_vma=False
    )
```
